256 devices in a mesh: row: 32 (over x, y, core), col: 8 (over z).
Axes of the slice: x: 4, y: 4, z: 8, core: 2. Of those that a mesh axis runs over, the one named last changes fastest.
Arguments:
- stored: float32 [16384, 4, 4096], P('row', None, 'col'), may hold values from -6 to 6
- panel: float32 [16384, 256], P('row', 'col'), may hold values from -620 to 620, as said below
Outputs:
- updated: float32 [16384, 4, 4096], P('row', None, 'col')
The draws below stay inside these ranges and needn't reach their ends.
Inputs may be any that keep to these rules, and one draw needn't show every extreme that they name: The panel has full column rank.
All inputs are finite; a program needn't handle non-finite values.
Results may differ from the reference program's by a relative error of at most 0.00007.
Values sent between devices are 32-bit elements; how exact they have to be, the bound alone decides.
A program may use at most 64 MiB of HBM per device.

```python
import math
import jax
import jax.numpy as jnp
from jax import lax

B = 512
K = 256
M = 16384
CT = 4
N_COL = 8


def draw_panel(key, part):
    key = jax.random.fold_in(key, 7)
    key_base, key_rows, key_cols = jax.random.split(key, 3)
    base = jnp.clip(jax.random.normal(key_base, (M, K), jnp.float32), -5.0, 5.0)
    position = jnp.arange(M, dtype=jnp.float32)[:, None] / M
    row_scale = (1.0 + position) * jnp.exp(jax.random.uniform(key_rows, (M, 1), jnp.float32, -0.5, 0.5))
    col_scale = jnp.exp(jax.random.uniform(key_cols, (1, K), jnp.float32, 0.0, math.log(10.0)))
    return base * row_scale * col_scale


def block_levels(rng, dims, pieces, smallest, top_value):
    def one(dim, parts):
        heights = jax.random.uniform(jax.random.fold_in(jax.random.fold_in(rng, 6), dim), (parts,), jnp.float32, smallest / len(pieces), top_value / len(pieces))
        return jnp.repeat(jnp.exp(heights), dims[dim] // parts).reshape((-1,) + (1,) * (len(dims) - dim - 1))

    level = one(*pieces[0])
    for cut in pieces[1:]:
        level = level * one(*cut)
    return level


def normal_values(key, extent, deviation, limit, shards=(), kind=jnp.bfloat16):
    drawn = deviation * jax.random.normal(key, extent, jnp.float32)
    if shards:
        drawn = drawn * block_levels(key, extent, shards, -0.22, 0.18)
    return jnp.clip(drawn, -limit, limit).astype(kind)


def setup_inputs(seed: int = 0) -> dict:
    key_of = jax.random.split(jax.random.key(seed), 3)
    stored = normal_values(key_of[0], (M, CT, N_COL * B), 1.0, 6.0, ((0, 32), (2, 8)), jnp.float32)
    panel = draw_panel(jax.random.fold_in(key_of[2], 71), 0)
    return {"stored": stored, "panel": panel}


def reference(stored, panel):
    highest = lax.Precision.HIGHEST
    order = stored.shape[0]
    full = stored.reshape(order, order)
    index = jnp.arange(order, dtype=jnp.int32)
    tile_of = index // B
    tile_rows = tile_of[:, None]
    tile_cols = tile_of[None, :]
    lower_keep = (tile_rows > tile_cols) | (tile_rows == tile_cols) & (index[:, None] >= index[None, :])
    strict_keep = (tile_rows > tile_cols) | (tile_rows == tile_cols) & (index[:, None] > index[None, :])
    symmetric = jnp.where(lower_keep, full, 0.0) + jnp.where(strict_keep, full, 0.0).T
    gram = jnp.dot(panel.T, panel, precision=highest)
    factor = jnp.linalg.cholesky(gram)
    basis = lax.linalg.triangular_solve(factor, panel, left_side=False, lower=True, transpose_a=True)
    product = jnp.dot(symmetric, basis, precision=highest)
    coupling = jnp.dot(basis.T, product, precision=highest)
    correction = 2.0 * product - 2.0 * jnp.dot(basis, coupling, precision=highest)
    transformed = symmetric - jnp.dot(basis, correction.T, precision=highest) - jnp.dot(correction, basis.T, precision=highest)
    result = jnp.where(tile_rows >= tile_cols, transformed, 0.0)
    return result.reshape(order, CT, N_COL * B)
```

```python
import functools

import jax
import jax.numpy as jnp
from jax import lax
from jax.experimental import pallas as pl
from jax.experimental.pallas import tpu as pltpu
from jax.sharding import PartitionSpec as P

F32 = jnp.float32
BF16 = jnp.bfloat16
HIGHEST = lax.Precision.HIGHEST
MESH = pl.DeviceIdType.MESH
TILE = 512
K = 256
SLOTS = 4
CHUNK = 64
WIDE = 80
NN = (((1,), (0,)), ((), ()))
NT = (((1,), (1,)), ((), ()))


def split(value):
    high = value.astype(BF16)
    return high, (value - high.astype(F32)).astype(BF16)


def dot3(left, right, dims=NN):
    (lh, ll), (rh, rl) = left, right
    dot = functools.partial(lax.dot_general, dimension_numbers=dims, preferred_element_type=F32)
    return dot(lh, rh) + (dot(lh, rl) + dot(ll, rh))


def dot6(left, right, dims=NN):
    return lax.dot_general(left, right, dims, precision=HIGHEST, preferred_element_type=F32)


def mod(value, size):
    return lax.rem(value, size)


class Place:
    def __init__(self):
        self.row = lax.axis_index("row")
        self.col = lax.axis_index("col")
        self.x = lax.div(self.row, 8)
        self.inner = mod(self.row, 8)
        self.y = lax.div(self.inner, 2)
        self.core = mod(self.row, 2)
        self.u = self.y * (1 - self.core) + self.x * self.core
        self.v = self.x * (1 - self.core) + self.y * self.core

    def ring(self, du, dv):
        u, v = mod(self.u + du, 4), mod(self.v + dv, 4)
        return (8 * v + 2 * u) * (1 - self.core) + (8 * u + 2 * v + 1) * self.core

    def at(self, du, dv):
        return {"row": self.ring(du, dv), "col": self.col}

    def sibling(self):
        return {"row": self.row + 1 - 2 * self.core, "col": self.col}

    def up(self, dz):
        return {"row": self.row, "col": mod(self.col + dz % 8, 8)}


class Links:
    def __init__(self, send, recv):
        self.send, self.recv = send, recv
        self.sent, self.slots = 0, 0
        self.pending = []

    def slot(self):
        self.slots += 1
        return self.slots - 1

    def copy(self, source, target, slot, device, send=0):
        return pltpu.make_async_remote_copy(
            src_ref=source,
            dst_ref=target,
            send_sem=self.send.at[send],
            recv_sem=self.recv.at[slot],
            device_id=device,
            device_id_type=MESH,
        )

    def start(self, source, target, slot, device, when=None):
        copy = self.copy(source, target, slot, device, self.sent)
        self.sent += 1
        if when is None:
            copy.start()
        else:
            pl.when(when)(copy.start)
        self.pending.append((copy, when))

    def wait(self, target, slot, device, when=None):
        copy = self.copy(target, target, slot, device)
        if when is None:
            copy.wait_recv()
        else:
            pl.when(when)(copy.wait_recv)

    def finish(self):
        for copy, when in self.pending:
            if when is None:
                copy.wait_send()
            else:
                pl.when(when)(copy.wait_send)
        self.pending = []


def plane_gather(place, links, buf, rows):
    first, second = pl.ds(0, rows // 2), pl.ds(rows // 2, rows // 2)
    near = {name: links.slot() for name in ("l", "r", "a", "b")}
    far = [{name: links.slot() for name in ("l", "r", "a", "b")} for _ in range(4)]
    across = [[links.slot() for _ in range(4)] for _ in range(4)]

    def whole(du, dv):
        return buf.at[place.ring(du, dv)]

    def half(du, dv, part):
        return buf.at[place.ring(du, dv), part]

    def send(ref, slot, du, dv):
        links.start(ref, ref, slot, place.at(du, dv))

    def to_sibling(du, dv):
        links.start(whole(du, dv), whole(du, dv), across[du][dv], place.sibling())

    def spread(du):
        send(whole(du, 0), far[du]["l"], 0, 1)
        send(whole(du, 0), far[du]["r"], 0, 3)
        to_sibling(du, 0)

    def middle(du):
        links.wait(whole(du, 3), far[du]["l"], place.at(0, 3))
        send(half(du, 3, first), far[du]["a"], 0, 1)
        to_sibling(du, 3)
        links.wait(whole(du, 1), far[du]["r"], place.at(0, 1))
        send(half(du, 1, second), far[du]["b"], 0, 3)
        to_sibling(du, 1)

    send(whole(0, 0), near["l"], 1, 0)
    send(whole(0, 0), near["r"], 3, 0)
    spread(0)
    yield
    links.wait(whole(3, 0), near["l"], place.at(3, 0))
    send(half(3, 0, first), near["a"], 1, 0)
    links.wait(whole(1, 0), near["r"], place.at(1, 0))
    send(half(1, 0, second), near["b"], 3, 0)
    spread(3)
    spread(1)
    yield
    middle(0)
    yield
    links.wait(half(2, 0, first), near["a"], place.at(3, 0))
    links.wait(half(2, 0, second), near["b"], place.at(1, 0))
    spread(2)
    yield
    middle(3)
    middle(1)
    yield
    middle(2)
    yield
    for du in (0, 3, 1, 2):
        links.wait(half(du, 2, first), far[du]["a"], place.at(0, 3))
        links.wait(half(du, 2, second), far[du]["b"], place.at(0, 1))
        to_sibling(du, 2)
    yield
    su = place.v
    sv = place.u
    for du in range(4):
        for dv in range(4):
            u, v = mod(su + du, 4), mod(sv + dv, 4)
            chunk = (8 * v + 2 * u) * place.core + (8 * u + 2 * v + 1) * (1 - place.core)
            links.wait(buf.at[chunk], across[du][dv], place.sibling())


def ring_gather(place, links, buf):
    rows = buf.shape[1]
    part = (pl.ds(0, rows // 2), pl.ds(rows // 2, rows // 2))
    slots = [(links.slot(), links.slot()) for _ in range(4)]

    def ref(offset, which, step):
        chunk = mod(place.col + offset % 8, 8)
        return buf.at[chunk, part[which]] if step == 3 else buf.at[chunk]

    for step in range(4):
        for which, way in ((0, 1), (1, 7)):
            if step:
                links.wait(ref(-way * step, which, step - 1), slots[step - 1][which], place.up(-way))
            source = ref(-way * step, which, step)
            links.start(source, source, slots[step][which], place.up(way))
        yield
    for which, way in ((0, 1), (1, 7)):
        links.wait(ref(4, which, 3), slots[3][which], place.up(-way))


def ring_sum(place, links, buf, land):
    rows = buf.shape[1]
    part = (pl.ds(0, rows // 2), pl.ds(rows // 2, rows // 2))
    slots = [(links.slot(), links.slot()) for _ in range(4)]
    for step in range(5):
        for which, way in ((0, 1), (1, 7)):
            chunk = mod(place.col + way * (4 - step) % 8, 8)
            if step:
                spot = land.at[which, step - 1, part[which]] if step == 1 else land.at[which, step - 1]
                links.wait(spot, slots[step - 1][which], place.up(-way))
                if step == 1:
                    buf[chunk, part[which]] += spot[...]
                else:
                    buf[chunk] += spot[...]
            if step < 4:
                source = buf.at[chunk, part[which]] if step == 0 else buf.at[chunk]
                spot = land.at[which, step, part[which]] if step == 0 else land.at[which, step]
                links.start(source, spot, slots[step][which], place.up(way))
        if step < 4:
            yield


def sibling_send(place, links, buf, land, slots, tile):
    for y in range(4):
        links.start(
            buf.at[8 * tile + 2 * y + 1 - place.core],
            land.at[4 * tile + y],
            slots[4 * tile + y],
            place.sibling(),
        )


def plane_sum(place, links, buf, sib, sib_slots, rb, rw, cb, cw):
    rows = buf.shape[1]
    part = (pl.ds(0, rows // 2), pl.ds(rows // 2, rows // 2))
    vb = [(links.slot(), links.slot()) for _ in range(4)]
    vw = [(links.slot(), links.slot()) for _ in range(4)]
    ub = (links.slot(), links.slot())
    uw = (links.slot(), links.slot())
    for index in range(16):
        links.wait(sib.at[index], sib_slots[index], place.sibling())

        buf[8 * (index // 4) + 2 * (index % 4) + place.core] += sib[index]
    order = (2, 1, 3, 0)
    for du in order:
        for which, way in ((0, 1), (1, 3)):
            links.start(
                buf.at[place.ring(du, 2), part[which]], rb.at[du, part[which]], vb[du][which], place.at(0, way)
            )
    yield
    for du in order:
        for which, way in ((0, 1), (1, 3)):
            links.wait(rb.at[du, part[which]], vb[du][which], place.at(0, 4 - way))
            chunk = place.ring(du, way)
            buf[chunk, part[which]] += rb[du, part[which]]
            links.start(buf.at[chunk], rw.at[which, du], vw[du][which], place.at(0, way))
    yield
    for du in order:
        for which, way in ((0, 1), (1, 3)):
            links.wait(rw.at[which, du], vw[du][which], place.at(0, 4 - way))
        chunk = place.ring(du, 0)
        buf[chunk] += rw[0, du] + rw[1, du]
        if du == 2:
            for which, way in ((0, 1), (1, 3)):
                links.start(buf.at[chunk, part[which]], cb.at[part[which]], ub[which], place.at(way, 0))
    yield
    for which, way in ((0, 1), (1, 3)):
        links.wait(cb.at[part[which]], ub[which], place.at(4 - way, 0))
        chunk = place.ring(way, 0)
        buf[chunk, part[which]] += cb[part[which]]
        links.start(buf.at[chunk], cw.at[which], uw[which], place.at(way, 0))
    yield
    for which, way in ((0, 1), (1, 3)):
        links.wait(cw.at[which], uw[which], place.at(4 - way, 0))
    buf[place.ring(0, 0)] += cw[0] + cw[1]


def unpack(pieces):
    lane = lax.broadcasted_iota(jnp.int32, (16, 128), 1) // 32
    bands = []
    for quarter in range(4):
        sides = []
        for side in range(2):
            out = None
            for group in range(4):
                piece = pieces[4 * side + group]
                shift = (group - quarter) * 32 % 128
                piece = pltpu.roll(piece, shift, 1) if shift else piece
                out = piece if out is None else jnp.where(lane == group, piece, out)
            sides.append(out)
        bands.append(jnp.concatenate(sides, 1))
    return jnp.concatenate(bands, 0)


def exchange_kernel(
    stored,
    panel,
    acol_hi_out,
    acol_lo_out,
    arow_hi_out,
    arow_lo_out,
    ycol_out,
    yrow_out,
    s,
    pk,
    colpk,
    rowpk,
    acol,
    arow,
    acol_hi,
    acol_lo,
    arow_hi,
    arow_lo,
    rows,
    diag,
    part,
    sib,
    rb,
    rw,
    cb,
    cw,
    zland,
    turned,
    small,
    ycol,
    yrow,
    load_sem,
    out_sem,
    send_sem,
    recv_sem,
):
    place = Place()
    links = Links(send_sem, recv_sem)
    row, col, inner = place.row, place.col, place.inner
    base = row - inner
    loads = [pltpu.make_async_copy(stored.at[:, k, :], s.at[k], load_sem.at[k]) for k in range(SLOTS)]
    for load in loads:
        load.start()

    barrier = pltpu.get_barrier_semaphore()

    def greet(device):
        pl.semaphore_signal(barrier, inc=1, device_id=device, device_id_type=MESH)

    own = inner == col
    turn = {"row": base + col, "col": inner}
    for step in range(1, 8):
        greet(place.up(step))
        greet({"row": base + mod(inner + step, 8), "col": inner})
        greet({"row": base + col, "col": mod(col + step, 8)})
    for device in (place.at(1, 0), place.at(3, 0), place.at(0, 1), place.at(0, 3), place.sibling()):
        greet(device)

    @pl.when(jnp.logical_not(own))
    def _():
        greet({"row": row, "col": inner})
        greet({"row": base + col, "col": col})

    for index in range(8):
        start = index * CHUNK
        pk[index] = jnp.concatenate(
            [panel[start + 16 * quarter : start + 16 * (quarter + 1), :] for quarter in range(4)], 1
        )
    other = jnp.logical_not(own)
    pl.when(own)(lambda: pl.semaphore_wait(barrier, 26))
    pl.when(other)(lambda: pl.semaphore_wait(barrier, 28))

    col_slot = links.slots
    row_slot = links.slots + 8
    links.slots += 16
    for step in range(8):
        piece = mod(inner + step, 8)
        links.start(
            pk.at[piece],
            colpk.at[col],
            col_slot + col,
            {"row": base + piece, "col": inner},
            None if step else other,
        )
    for step in range(1, 8):
        piece = mod(col + step, 8)
        links.start(pk.at[piece], rowpk.at[col], row_slot + col, place.up(step))
    rowpk[col] = pk[col]

    @pl.when(own)
    def _():
        colpk[col] = pk[inner]

    for step in range(8):
        piece = mod(col + step, 8)
        device = {"row": base + col, "col": piece}
        links.wait(colpk.at[piece], col_slot + piece, device, None if step else other)
        if step:
            links.wait(rowpk.at[piece], row_slot + piece, place.up(step))
    acol[row] = unpack([colpk[index] for index in range(8)])
    arow[col] = unpack([rowpk[index] for index in range(8)])

    wide = plane_gather(place, links, acol, CHUNK)
    deep = ring_gather(place, links, arow)
    next(wide)
    next(deep)
    chunk = acol[row]
    gram = dot6(chunk.T, chunk)
    part[:, CHUNK : CHUNK + 8, :] = gram.reshape(32, 8, K)
    next(wide)
    next(deep)
    for load in loads:
        load.wait()

    @pl.when(own)
    def _():
        value = s[place.x]
        below = lax.broadcasted_iota(jnp.int32, (TILE, TILE), 0)
        across = lax.broadcasted_iota(jnp.int32, (TILE, TILE), 1)
        s[place.x] = jnp.where(below >= across, value, 0.0) + jnp.where(below > across, value, 0.0).T

    next(wide)
    next(deep)
    next(wide)
    next(deep)
    for _ in deep:
        pass
    for _ in wide:
        pass

    def store_halves(source, high, low, outs, sems):
        high[...], low[...] = split(source[...])
        copies = [pltpu.make_async_copy(ref, out, out_sem.at[sem]) for ref, out, sem in zip((high, low), outs, sems)]
        for copy in copies:
            copy.start()
        return copies

    copies = store_halves(arow, arow_hi, arow_lo, (arow_hi_out, arow_lo_out), (0, 1))
    copies += store_halves(acol, acol_hi, acol_lo, (acol_hi_out, acol_lo_out), (2, 3))

    rows[...] = jnp.zeros_like(rows)
    diag[...] = jnp.zeros_like(diag)

    def row_terms(k, carry):
        @pl.when(8 * k + col < row)
        def _():
            right = [ref[pl.ds(8 * k, 8)].reshape(TILE, K) for ref in (acol_hi, acol_lo)]
            rows[...] += dot3(split(s[k]), right).reshape(rows.shape)

        return carry

    lax.fori_loop(0, SLOTS, row_terms, 0)
    arow_halves = [ref[...].reshape(TILE, K) for ref in (arow_hi, arow_lo)]

    @pl.when(own)
    def _():
        diag[...] = dot3(split(s[place.x]), arow_halves).reshape(diag.shape)

    terms = (rows[...] + 0.5 * diag[...]).reshape(TILE, K)
    lower = dot3(split(arow[...].reshape(TILE, K).T), split(terms))
    part[:, CHUNK + 8 :, :] = lower.reshape(32, 8, K)
    rows[...] += diag[...]

    deep = ring_sum(place, links, rows, zland)
    next(deep)
    sib_slots = [links.slot() for _ in range(16)]
    for k in range(SLOTS):
        part[8 * k : 8 * k + 8, :CHUNK, :] = jnp.zeros((8, CHUNK, K), F32)

        @pl.when(8 * k + col < row)
        def _():
            terms = dot3(split(s[k].T), [ref[...].reshape(TILE, K) for ref in (arow_hi, arow_lo)])
            part[8 * k : 8 * k + 8, :CHUNK, :] = terms.reshape(8, CHUNK, K)

        sibling_send(place, links, part, sib, sib_slots, k)
        if k < SLOTS - 1:
            next(deep)
    wide = plane_sum(place, links, part, sib, sib_slots, rb, rw, cb, cw)
    next(wide)
    for _ in deep:
        pass

    turn_slot = links.slot()
    links.start(rows.at[col], turned, turn_slot, turn, other)

    @pl.when(own)
    def _():
        turned[...] = rows[col]

    for _ in wide:
        pass
    small_slot = links.slots
    links.slots += 8
    small[col] = part[row, CHUNK:, :]
    for step in range(1, 8):
        links.start(part.at[row, pl.ds(CHUNK, 16)], small.at[col], small_slot + col, place.up(step))
    links.wait(turned, turn_slot, turn, other)
    product = part[row, :CHUNK, :] + turned[...]
    ycol[row, :CHUNK, :] = product
    back_slot = links.slot()
    links.start(ycol.at[row, pl.ds(0, CHUNK)], yrow.at[inner], back_slot, turn, other)

    @pl.when(own)
    def _():
        yrow[inner] = product

    for step in range(1, 8):
        piece = mod(col + step, 8)
        links.wait(small.at[piece], small_slot + piece, place.up(step))
    ycol[row, CHUNK:, :] = jnp.sum(small[...], 0)
    wide = plane_gather(place, links, ycol, WIDE)
    deep = ring_gather(place, links, yrow)
    next(wide)
    links.wait(yrow.at[col], back_slot, turn, other)
    next(deep)
    next(wide)
    next(deep)
    next(wide)
    next(deep)
    next(wide)
    next(deep)
    for _ in deep:
        pass
    for _ in wide:
        pass
    copies += [
        pltpu.make_async_copy(ref, out, out_sem.at[sem])
        for ref, out, sem in ((ycol, ycol_out, 4), (yrow, yrow_out, 5))
    ]
    copies[-2].start()
    copies[-1].start()
    for copy in copies:
        copy.wait()
    links.finish()


def update_kernel(
    stored, acol_hi, acol_lo, arow_hi, arow_lo, ycol, yrow, out, s, ah, al, rh, rl, yc, yr, gn, inv, scaled_ref, load_sem, out_sem
):
    row, col = lax.axis_index("row"), lax.axis_index("col")
    first = pltpu.make_async_copy(ycol.at[:, pl.ds(CHUNK, 16), :], gn, load_sem.at[0])
    first.start()
    loads = [
        pltpu.make_async_copy(source, target, load_sem.at[index + 1])
        for index, (source, target) in enumerate(
            [(yrow, yr), (arow_hi, rh), (arow_lo, rl), (ycol.at[:, pl.ds(0, CHUNK), :], yc), (acol_hi, ah), (acol_lo, al)]
            + [(stored.at[:, k, :], s.at[k]) for k in range(SLOTS)]
        )
    ]
    for load in loads:
        load.start()
    first.wait()
    gram = gn[:, :8, :].reshape(K, K)
    lower = gn[:, 8:, :].reshape(K, K)
    across = lax.broadcasted_iota(jnp.int32, (K, K), 1)
    eye = lax.broadcasted_iota(jnp.int32, (K, K), 0) == across
    diagonal = jnp.where(eye, gram, 0.0)
    left = lax.rsqrt(jnp.sum(diagonal, 1, keepdims=True))
    right = lax.rsqrt(jnp.sum(diagonal, 0, keepdims=True))
    scaled = gram * left * right
    unit = jnp.where(eye, 1.0, 0.0)
    rest = unit - scaled
    square = dot3(split(rest), split(rest))
    close = jnp.sum(square * square) < 0.25
    bound = jnp.max(jnp.sum(jnp.abs(scaled), 1, keepdims=True))
    inv[...] = jnp.where(close, unit + rest, unit / bound)
    scaled_ref[...] = scaled

    def again(state):
        count, size = state
        return (count < 64) & (size > 1e-6)

    def refine(state):
        count, _ = state
        value = inv[...]
        rest = unit - dot6(scaled_ref[...], value)
        inv[...] = value + dot3(split(value), split(rest))
        return count + 1, jnp.sum(rest * rest)

    lax.while_loop(again, refine, (jnp.int32(0), jnp.float32(1.0)))
    inverse = inv[...] * left * right
    coupling = lower + lower.T
    halves = split(inverse)
    twist = dot3(halves, split(dot3(split(coupling), halves)))
    mix = split(jnp.concatenate([2.0 * inverse, -2.0 * twist], 0))
    for load in loads[:3]:
        load.wait()
    row_halves = rh[...], rl[...]
    yr_halves = split(yr[...].reshape(TILE, K))
    row_halves = [ref[...].reshape(TILE, K) for ref in (rh, rl)]
    wrow = split(dot3([jnp.concatenate(pair, 1) for pair in zip(yr_halves, row_halves)], mix))
    left_pair = [jnp.concatenate(pair, 1) for pair in zip(row_halves, wrow)]
    for load in loads[3:6]:
        load.wait()
    stores = []
    for k in range(SLOTS):
        loads[6 + k].wait()

        @pl.when(8 * k + col == row)
        def _():
            value = s[k]
            down = lax.broadcasted_iota(jnp.int32, (TILE, TILE), 0)
            along = lax.broadcasted_iota(jnp.int32, (TILE, TILE), 1)
            s[k] = jnp.where(down >= along, value, 0.0) + jnp.where(down > along, value, 0.0).T

        @pl.when(8 * k + col > row)
        def _():
            s[k] = jnp.zeros((TILE, TILE), F32)

        @pl.when(8 * k + col <= row)
        def _():
            y_halves = split(yc[8 * k : 8 * k + 8].reshape(TILE, K))
            a_halves = [ref[8 * k : 8 * k + 8].reshape(TILE, K) for ref in (ah, al)]
            wcol = split(dot3([jnp.concatenate(pair, 1) for pair in zip(y_halves, a_halves)], mix))
            right_pair = [jnp.concatenate(pair, 1) for pair in zip(wcol, a_halves)]
            s[k] -= dot3(left_pair, right_pair, NT)

        stores.append(pltpu.make_async_copy(s.at[k], out.at[:, k, :], out_sem.at[k]))
        stores[-1].start()
    for store in stores:
        store.wait()


def body(stored, panel):
    any_spec = pl.BlockSpec(memory_space=pl.ANY)
    col_bf = jax.ShapeDtypeStruct((32, CHUNK, K), BF16)
    row_bf = jax.ShapeDtypeStruct((8, CHUNK, K), BF16)
    vmem, dma = pltpu.VMEM, pltpu.SemaphoreType.DMA
    outs = (
        col_bf,
        col_bf,
        row_bf,
        row_bf,
        jax.ShapeDtypeStruct((32, WIDE, K), F32),
        jax.ShapeDtypeStruct((8, CHUNK, K), F32),
    )
    parts = pl.pallas_call(
        exchange_kernel,
        out_shape=outs,
        in_specs=[any_spec, pl.BlockSpec(memory_space=pltpu.VMEM)],
        out_specs=[any_spec] * 6,
        scratch_shapes=[
            vmem((SLOTS, TILE, TILE), F32),
            vmem((8, 16, 128), F32),
            vmem((8, 16, 128), F32),
            vmem((8, 16, 128), F32),
            vmem((32, CHUNK, K), F32),
            vmem((8, CHUNK, K), F32),
            vmem((32, CHUNK, K), BF16),
            vmem((32, CHUNK, K), BF16),
            vmem((8, CHUNK, K), BF16),
            vmem((8, CHUNK, K), BF16),
            vmem((8, CHUNK, K), F32),
            vmem((8, CHUNK, K), F32),
            vmem((32, WIDE, K), F32),
            vmem((16, WIDE, K), F32),
            vmem((4, WIDE, K), F32),
            vmem((2, 4, WIDE, K), F32),
            vmem((WIDE, K), F32),
            vmem((2, WIDE, K), F32),
            vmem((2, 4, CHUNK, K), F32),
            vmem((CHUNK, K), F32),
            vmem((8, 16, K), F32),
            vmem((32, WIDE, K), F32),
            vmem((8, CHUNK, K), F32),
            dma((SLOTS,)),
            dma((6,)),
            dma((220,)),
            dma((220,)),
        ],
        compiler_params=pltpu.CompilerParams(
            collective_id=0, has_side_effects=True, vmem_limit_bytes=56 << 20
        ),
        name="exchange",
    )(stored, panel)
    return pl.pallas_call(
        update_kernel,
        out_shape=jax.ShapeDtypeStruct(stored.shape, F32),
        in_specs=[any_spec] * 7,
        out_specs=any_spec,
        scratch_shapes=[
            vmem((SLOTS, TILE, TILE), F32),
            vmem((32, CHUNK, K), BF16),
            vmem((32, CHUNK, K), BF16),
            vmem((8, CHUNK, K), BF16),
            vmem((8, CHUNK, K), BF16),
            vmem((32, CHUNK, K), F32),
            vmem((8, CHUNK, K), F32),
            vmem((32, 16, K), F32),
            vmem((K, K), F32),
            vmem((K, K), F32),
            dma((11,)),
            dma((SLOTS,)),
        ],
        compiler_params=pltpu.CompilerParams(vmem_limit_bytes=56 << 20),
        name="update",
    )(stored, *parts)


def solution(mesh):
    in_specs = (P("row", None, "col"), P("row", "col"))
    out_specs = P("row", None, "col")
    return jax.shard_map(body, mesh=mesh, in_specs=in_specs, out_specs=out_specs, check_vma=False)
```

```python
import functools

import jax
import jax.numpy as jnp
from jax import lax
from jax.experimental import pallas as pl
from jax.experimental.pallas import tpu as pltpu
from jax.sharding import PartitionSpec as P

F32 = jnp.float32
BF16 = jnp.bfloat16
HIGHEST = lax.Precision.HIGHEST
MESH = pl.DeviceIdType.MESH
TILE = 512
K = 256
SLOTS = 4
SENDS, RECVS = 22, 54
CHUNK = 64
NN = (((1,), (0,)), ((), ()))
NT = (((1,), (1,)), ((), ()))


def split(value):
    high = value.astype(BF16)
    return high, (value - high.astype(F32)).astype(BF16)


def dot3(left, right, dims=NN):
    (lh, ll), (rh, rl) = left, right
    dot = functools.partial(lax.dot_general, dimension_numbers=dims, preferred_element_type=F32)
    return dot(lh, rh) + (dot(lh, rl) + dot(ll, rh))


def dot6(left, right, dims=NN):
    return lax.dot_general(left, right, dims, precision=HIGHEST, preferred_element_type=F32)


def mod(value, size):
    return lax.rem(value, size)


class Place:
    def __init__(self):
        self.row = lax.axis_index("row")
        self.col = lax.axis_index("col")
        self.x = lax.div(self.row, 8)
        self.inner = mod(self.row, 8)
        self.y = lax.div(self.inner, 2)
        self.core = mod(self.row, 2)
        self.u = self.y * (1 - self.core) + self.x * self.core
        self.v = self.x * (1 - self.core) + self.y * self.core

    def ring(self, du, dv):
        u, v = mod(self.u + du, 4), mod(self.v + dv, 4)
        return (8 * v + 2 * u) * (1 - self.core) + (8 * u + 2 * v + 1) * self.core

    def at(self, du, dv):
        return {"row": self.ring(du, dv), "col": self.col}

    def sibling(self):
        return {"row": self.row + 1 - 2 * self.core, "col": self.col}

    def up(self, dz):
        return {"row": self.row, "col": mod(self.col + dz % 8, 8)}


class Links:
    def __init__(self, send, recv):
        self.send, self.recv = send, recv
        self.sends, self.slots = 0, 0
        self.ends = []

    def slot(self):
        self.slots += 1
        return self.slots - 1

    def batch(self, ref, when=None):
        self.sends += 1
        self.ends.append((self.sends - 1, ref, when))
        return self.sends - 1

    def copy(self, source, target, slot, device, send):
        return pltpu.make_async_remote_copy(
            src_ref=source,
            dst_ref=target,
            send_sem=self.send.at[send],
            recv_sem=self.recv.at[slot],
            device_id=device,
            device_id_type=MESH,
        )

    def start(self, source, target, slot, device, send=None, when=None):
        send = self.batch(source) if send is None else send
        copy = self.copy(source, target, slot, device, send)
        copy.start() if when is None else pl.when(when)(copy.start)

    def wait(self, ref, slot, device, when=None):
        copy = self.copy(ref, ref, slot, device, 0)
        copy.wait_recv() if when is None else pl.when(when)(copy.wait_recv)

    def finish(self, device):
        for send, ref, when in self.ends:
            copy = self.copy(ref, ref, 0, device, send)
            copy.wait_send() if when is None else pl.when(when)(copy.wait_send)


def plane_gather(place, links, buf):
    near = [None] + [links.slot() for _ in range(3)]
    far = [links.slot() for _ in range(4)]
    across = links.slot()
    batch = links.batch(buf.at[pl.ds(0, 31)])

    def send(du, dv, slot, device):
        ref = buf.at[place.ring(du, dv)]
        links.start(ref, ref, slot, device, batch)

    def spread(du):
        for way in (2, 1, 3):
            send(du, 0, far[du], place.at(0, way))
        send(du, 0, across, place.sibling())

    for way in (2, 1, 3):
        send(0, 0, near[way], place.at(way, 0))
    spread(0)
    yield
    for way in (1, 3, 2):
        links.wait(buf.at[place.ring(4 - way, 0)], near[way], place.at(4 - way, 0))
        spread(4 - way)
        yield
    for du in (0, 3, 1, 2):
        links.wait(buf.at[pl.ds(0, 3)], far[du], place.at(0, 1))
        for way in (1, 3, 2):
            send(du, way, across, place.sibling())
        yield
    links.wait(buf.at[pl.ds(0, 16)], across, place.sibling())


def plane_sum(place, links, buf, sib, vland, uland):
    sib_slots = [links.slot() for _ in range(SLOTS)]
    vs = [links.slot() for _ in range(4)]
    us = links.slot()
    batch = links.batch(buf.at[pl.ds(0, 31)])
    for tile in range(SLOTS):
        for y in range(4):
            links.start(
                buf.at[8 * tile + 2 * y + 1 - place.core],
                sib.at[4 * tile + y],
                sib_slots[tile],
                place.sibling(),
                batch,
            )
        yield
    for tile in range(SLOTS):
        links.wait(sib.at[pl.ds(4 * tile, 4)], sib_slots[tile], place.sibling())
        for y in range(4):
            buf[8 * tile + 2 * y + place.core] += sib[4 * tile + y]
    order = (2, 1, 3, 0)
    for du in order:
        for way in (2, 1, 3):
            links.start(buf.at[place.ring(du, way)], vland.at[du, way - 1], vs[du], place.at(0, way), batch)
    yield
    for du in order:
        links.wait(vland.at[du], vs[du], place.at(0, 1))
        chunk = place.ring(du, 0)
        buf[chunk] += vland[du, 0] + (vland[du, 1] + vland[du, 2])
        if du:
            links.start(buf.at[chunk], uland.at[du - 1], us, place.at(du, 0), batch)
        yield
    links.wait(uland, us, place.at(1, 0))
    buf[place.ring(0, 0)] += uland[0] + (uland[1] + uland[2])


def small_sum(place, links, value, sib, chips, depth, total):
    chip = lax.div(place.row, 2)
    sib_slot, chip_slot, depth_slot, back_slot, last_slot = [links.slot() for _ in range(5)]

    def peer(step):
        index = mod(chip + step, 16)
        return index, {"row": 2 * index + place.core, "col": place.col}

    links.start(value.at[:, 1 - place.core], sib, sib_slot, place.sibling())
    yield
    links.wait(sib, sib_slot, place.sibling())
    for index in range(16):
        chips[index] = value[index, place.core] + sib[index]
    batch = links.batch(chips.at[pl.ds(0, 15)])
    for step in range(1, 16):
        index, device = peer(step)
        links.start(chips.at[index], depth.at[0, chip], chip_slot, device, batch)
    yield
    links.wait(depth.at[0, pl.ds(0, 15)], chip_slot, place.sibling())
    depth[0, chip] = chips[chip]
    depth[1, place.col] = jnp.sum(depth[0], 0)
    batch = links.batch(depth.at[1, pl.ds(0, 7)])
    for step in range(1, 8):
        links.start(depth.at[1, place.col], depth.at[1, place.col], depth_slot, place.up(step), batch)
    yield
    links.wait(depth.at[1, pl.ds(0, 7)], depth_slot, place.up(1))
    total[chip, place.core] = jnp.sum(depth[1, :8], 0)
    own = total.at[chip, place.core]
    batch = links.batch(total.at[pl.ds(0, 15), place.core])
    for step in range(1, 16):
        links.start(own, own, back_slot, peer(step)[1], batch)
    yield
    links.wait(total.at[pl.ds(0, 15), place.core], back_slot, place.sibling())
    links.start(total.at[:, place.core], total.at[:, place.core], last_slot, place.sibling())
    yield
    links.wait(total.at[:, 1 - place.core], last_slot, place.sibling())


def ring_gather(place, links, buf):
    rows = buf.shape[1]
    part = (pl.ds(0, rows // 2), pl.ds(rows // 2, rows // 2))
    one, two, three, four = [(links.slot(), links.slot()) for _ in range(4)]
    wholes, halves = links.batch(buf.at[pl.ds(0, 6)]), links.batch(buf.at[0])
    ways = ((0, 1), (1, -1))

    def piece(offset):
        return buf.at[mod(place.col + offset % 8, 8)]

    def half(offset, which):
        return buf.at[mod(place.col + offset % 8, 8), part[which]]

    for which, way in ways:
        links.start(piece(0), piece(0), two[which], place.up(2 * way), wholes)
    for which, way in ways:
        links.start(piece(0), piece(0), one[which], place.up(way), wholes)
    yield
    for which, way in ways:
        source = piece(-2 * way)
        links.wait(source, two[which], place.up(-2 * way))
        links.start(half(-2 * way, which), half(-2 * way, which), four[which], place.up(2 * way), halves)
        links.start(source, source, three[which], place.up(way), wholes)
    yield
    for which, way in ways:
        links.wait(piece(-way), one[which], place.up(-way))
        links.wait(piece(-3 * way), three[which], place.up(-way))
        links.wait(half(-4 * way, which), four[which], place.up(-2 * way))


def ring_sum(place, links, buf, land, half_land):
    rows = buf.shape[1]
    part = (pl.ds(0, rows // 2), pl.ds(rows // 2, rows // 2))
    one, two, three, four = [(links.slot(), links.slot()) for _ in range(4)]
    wholes, halves = links.batch(buf.at[pl.ds(0, 6)]), links.batch(buf.at[0])
    ways = ((0, 1), (1, -1))

    def piece(offset):
        return mod(place.col + offset % 8, 8)

    for which, way in ways:
        links.start(buf.at[piece(4 * way), part[which]], half_land.at[which], four[which], place.up(2 * way), halves)
        links.start(buf.at[piece(3 * way)], land.at[which, 2], three[which], place.up(way), wholes)
    for which, way in ways:
        links.start(buf.at[piece(way)], land.at[which, 0], one[which], place.up(way), wholes)
    yield
    for which, way in ways:
        links.wait(land.at[which, 2], three[which], place.up(-way))
        links.wait(half_land.at[which], four[which], place.up(-2 * way))
        index = piece(2 * way)
        buf[index] += land[which, 2]
        buf[index, part[which]] += half_land[which]
        links.start(buf.at[index], land.at[which, 1], two[which], place.up(2 * way), wholes)
    yield
    for which, way in ways:
        links.wait(land.at[which, 0], one[which], place.up(-way))
        links.wait(land.at[which, 1], two[which], place.up(-2 * way))
    buf[place.col] += (land[0, 0] + land[1, 0]) + (land[0, 1] + land[1, 1])


class Group:
    def __init__(self, place, links, source, target):
        self.place, self.links, self.source, self.target = place, links, source, target
        self.slot = links.slot()
        self.batch = links.batch(target.at[pl.ds(0, 7)])

    def send(self, index):
        place = self.place
        here = place.inner == index

        @pl.when(here)
        def _():
            self.target[place.inner] = self.source[index]

        device = {"row": place.row - place.inner + index, "col": place.col}
        self.links.start(
            self.source.at[index], self.target.at[place.inner], self.slot, device, self.batch, jnp.logical_not(here)
        )

    def wait(self):
        self.links.wait(self.target.at[pl.ds(0, 7)], self.slot, self.place.sibling())


class Turn:
    def __init__(self, place, links, target, own, other):
        self.place, self.links, self.target, self.own, self.other = place, links, target, own, other
        self.slot = links.slot()
        self.batches = links.batch(target.at[pl.ds(0, 7)], own), links.batch(target.at[pl.ds(0, 8)], other)

    def start(self, source, target, device, when):
        for batch, side in zip(self.batches, (self.own, self.other)):
            if when is None:
                self.links.start(source, target, self.slot, device, batch, side)
            elif side is self.other:
                self.links.start(source, target, self.slot, device, batch, side)

    def wait(self):
        self.links.wait(self.target.at[pl.ds(0, 7)], self.slot, self.place.sibling(), self.own)
        self.links.wait(self.target.at[pl.ds(0, 8)], self.slot, self.place.sibling(), self.other)


def unit_matrix():
    return jnp.where(
        lax.broadcasted_iota(jnp.int32, (K, K), 0) == lax.broadcasted_iota(jnp.int32, (K, K), 1), 1.0, 0.0
    ).astype(F32)


def scale(gram):
    diagonal = gram * unit_matrix()
    left = lax.rsqrt(jnp.sum(diagonal, 1, keepdims=True))
    right = lax.rsqrt(jnp.sum(diagonal, 0, keepdims=True))
    return gram * left * right, left, right


def refine(scaled, inverse):
    rest = unit_matrix() - dot6(scaled, inverse)
    return inverse + dot3(split(inverse), split(rest)), jnp.sum(rest * rest)


def mixing(inverse, lower):
    halves = split(inverse)
    twist = dot3(halves, split(dot3(split(lower + lower.T), halves)))
    return split(jnp.concatenate([2.0 * inverse, -2.0 * twist], 0))


def unpack(pieces):
    lane = lax.broadcasted_iota(jnp.int32, (16, 128), 1) // 32
    bands = []
    for quarter in range(4):
        sides = []
        for side in range(2):
            out = None
            for group in range(4):
                piece = pieces[4 * side + group]
                shift = (group - quarter) * 32 % 128
                piece = pltpu.roll(piece, shift, 1) if shift else piece
                out = piece if out is None else jnp.where(lane == group, piece, out)
            sides.append(out)
        bands.append(jnp.concatenate(sides, 1))
    return jnp.concatenate(bands, 0)


def exchange_kernel(
    stored,
    panel,
    acol_hi_out,
    acol_lo_out,
    arow_hi_out,
    arow_lo_out,
    ycol_out,
    yrow_out,
    gram_out,
    lower_out,
    mix_hi_out,
    mix_lo_out,
    size_out,
    s,
    flat,
    packed,
    colpk,
    acol,
    arow,
    acol_hi,
    acol_lo,
    arow_hi,
    arow_lo,
    rows,
    diag,
    whole,
    swapped,
    zland,
    zhalf,
    part,
    sib,
    vland,
    uland,
    ycol,
    yrow,
    gvalue,
    gsib,
    gchips,
    gdepth,
    gtotal,
    nvalue,
    nsib,
    nchips,
    ndepth,
    ntotal,
    scaled,
    inverse,
    mix_hi,
    mix_lo,
    size,
    load_sem,
    out_sem,
    send_sem,
    recv_sem,
):
    place = Place()
    links = Links(send_sem, recv_sem)
    row, col, inner = place.row, place.col, place.inner
    base = row - inner
    fetch = pltpu.make_async_copy(panel, flat, load_sem.at[SLOTS])
    fetch.start()
    loads = [pltpu.make_async_copy(stored.at[:, k, :], s.at[k], load_sem.at[k]) for k in range(SLOTS)]
    for load in loads:
        load.start()

    barrier = pltpu.get_barrier_semaphore()

    def greet(device):
        pl.semaphore_signal(barrier, inc=1, device_id=device, device_id_type=MESH)

    own = inner == col
    other = jnp.logical_not(own)
    for step in range(1, 8):
        greet({"row": base + mod(inner + step, 8), "col": inner})
        greet({"row": base + col, "col": mod(col + step, 8)})
        greet(place.up(step))
        greet({"row": base + mod(inner + step, 8), "col": col})
    for step in range(1, 16):
        greet({"row": mod(row + 2 * step, 32), "col": col})

    @pl.when(other)
    def _():
        greet({"row": row, "col": inner})
        greet({"row": base + col, "col": col})

    fetch.wait()
    for index in range(8):
        start = index * CHUNK
        packed[col, index] = jnp.concatenate(
            [flat[start + 16 * quarter : start + 16 * (quarter + 1), :] for quarter in range(4)], 1
        )
    pl.when(own)(lambda: pl.semaphore_wait(barrier, 43))
    pl.when(other)(lambda: pl.semaphore_wait(barrier, 45))

    turn = Turn(place, links, colpk, own, other)
    for step in range(8):
        piece = mod(inner + step, 8)
        device = {"row": base + piece, "col": inner}
        turn.start(packed.at[col, piece], colpk.at[col], device, None if step else other)
    deep = ring_gather(place, links, packed)
    next(deep)

    @pl.when(own)
    def _():
        colpk[col] = packed[col, inner]

    for load in loads:
        load.wait()

    @pl.when(own)
    def _():
        value = s[place.x]
        below = lax.broadcasted_iota(jnp.int32, (TILE, TILE), 0)
        across = lax.broadcasted_iota(jnp.int32, (TILE, TILE), 1)
        s[place.x] = jnp.where(below >= across, value, 0.0) + jnp.where(below > across, value, 0.0).T

    next(deep)
    turn.wait()
    acol[row] = unpack([colpk[index] for index in range(8)])
    wide = plane_gather(place, links, acol)
    next(wide)
    chunk = acol[row]
    gvalue[...] = dot6(chunk.T, chunk).reshape(gvalue.shape)
    gsum = small_sum(place, links, gvalue, gsib, gchips, gdepth, gtotal)
    next(gsum)
    for _ in deep:
        pass
    for _ in range(3):
        next(wide)

    def unpack_row(index, carry):
        arow[index] = unpack([packed[piece, index] for piece in range(8)])
        return carry

    lax.fori_loop(0, 8, unpack_row, 0)

    def store_halves(source, high, low, outs, sems):
        high[...], low[...] = split(source[...])
        copies = [pltpu.make_async_copy(ref, out, out_sem.at[sem]) for ref, out, sem in zip((high, low), outs, sems)]
        for copy in copies:
            copy.start()
        return copies

    copies = store_halves(arow, arow_hi, arow_lo, (arow_hi_out, arow_lo_out), (0, 1))
    next(gsum)
    next(wide)

    tall = plane_sum(place, links, part, sib, vland, uland)
    for k in range(SLOTS):
        part[8 * k : 8 * k + 8] = jnp.zeros((8, CHUNK, K), F32)

        @pl.when(8 * k + col < row)
        def _():
            terms = dot3(split(s[k].T), [ref[...].reshape(TILE, K) for ref in (arow_hi, arow_lo)])
            part[8 * k : 8 * k + 8] = terms.reshape(8, CHUNK, K)

        next(tall)
        if k < 3:
            next(wide)
    next(tall)
    next(gsum)
    for _ in wide:
        pass
    copies += store_halves(acol, acol_hi, acol_lo, (acol_hi_out, acol_lo_out), (2, 3))

    rows[...] = jnp.zeros_like(rows)
    diag[...] = jnp.zeros_like(diag)
    group = Group(place, links, whole, swapped)
    for block in range(2):
        chunks = pl.ds(4 * block, 4)
        span = pl.ds(TILE // 2 * block, TILE // 2)

        def row_terms(k, carry):
            @pl.when(8 * k + col < row)
            def _():
                right = [ref[pl.ds(8 * k, 8)].reshape(TILE, K) for ref in (acol_hi, acol_lo)]
                rows[chunks] += dot3(split(s[k, span]), right).reshape(4, CHUNK, K)

            return carry

        lax.fori_loop(0, SLOTS, row_terms, 0)

        @pl.when(own)
        def _():
            right = [ref[...].reshape(TILE, K) for ref in (arow_hi, arow_lo)]
            diag[chunks] = dot3(split(s[place.x, span]), right).reshape(4, CHUNK, K)

        whole[chunks] = rows[chunks] + diag[chunks]
        for index in range(4 * block, 4 * block + 4):
            group.send(index)

    terms = (rows[...] + 0.5 * diag[...]).reshape(TILE, K)
    lower = dot3(split(arow[...].reshape(TILE, K).T), split(terms))
    nvalue[...] = lower.reshape(nvalue.shape)
    nsum = small_sum(place, links, nvalue, nsib, nchips, ndepth, ntotal)
    next(nsum)
    next(gsum)
    next(tall)
    next(nsum)
    group.wait()
    deep = ring_sum(place, links, swapped, zland, zhalf)
    next(deep)
    for _ in range(3):
        next(tall)
    next(gsum)
    next(deep)
    next(nsum)
    for _ in tall:
        pass
    for _ in gsum:
        pass
    scaled[...], left, right = scale(gtotal[...].reshape(K, K))
    rest = unit_matrix() - scaled[...]
    square = dot3(split(rest), split(rest))
    close = jnp.sum(square * square) < 0.25
    bound = jnp.max(jnp.sum(jnp.abs(scaled[...]), 1, keepdims=True))
    inverse[...] = jnp.where(close, unit_matrix() + rest, unit_matrix() / bound)
    for _ in deep:
        pass
    product = part[row] + swapped[col]
    ycol[row] = product

    wide = plane_gather(place, links, ycol)
    next(wide)
    turn = Turn(place, links, yrow, own, other)
    for step in range(8):
        piece = mod(col + step, 8)
        device = {"row": base + col, "col": piece}
        turn.start(ycol.at[row], yrow.at[inner], device, None if step else other)

    @pl.when(own)
    def _():
        yrow[inner] = product

    next(nsum)
    inverse[...], _ = refine(scaled[...], inverse[...])
    for _ in range(3):
        next(wide)
    next(nsum)
    inverse[...], _ = refine(scaled[...], inverse[...])
    next(wide)
    inverse[...], _ = refine(scaled[...], inverse[...])
    next(wide)
    inverse[...], final = refine(scaled[...], inverse[...])
    size[...] = jnp.full(size.shape, final, F32)
    next(wide)
    for _ in nsum:
        pass
    mix_hi[...], mix_lo[...] = mixing(inverse[...] * left * right, ntotal[...].reshape(K, K))
    next(wide)
    turn.wait()
    for _ in wide:
        pass
    ends = ((ycol, ycol_out), (yrow, yrow_out), (gtotal, gram_out), (ntotal, lower_out))
    ends += ((mix_hi, mix_hi_out), (mix_lo, mix_lo_out), (size, size_out))
    last = [pltpu.make_async_copy(ref, out, out_sem.at[4 + index]) for index, (ref, out) in enumerate(ends)]
    for copy in last:
        copy.start()
    for copy in copies + last:
        copy.wait()
    links.finish(place.sibling())


def update_kernel(
    stored,
    acol_hi,
    acol_lo,
    arow_hi,
    arow_lo,
    ycol,
    yrow,
    gram_in,
    lower_in,
    mix_hi,
    mix_lo,
    size_in,
    out,
    s,
    ah,
    al,
    rh,
    rl,
    yc,
    yr,
    gn,
    mh,
    ml,
    size,
    scaled,
    inverse,
    load_sem,
    out_sem,
):
    row, col = lax.axis_index("row"), lax.axis_index("col")
    pairs = [(size_in, size), (mix_hi, mh), (mix_lo, ml), (yrow, yr), (arow_hi, rh), (arow_lo, rl)]
    pairs += [(gram_in, gn.at[0]), (lower_in, gn.at[1])]
    heads = len(pairs)
    for k in range(SLOTS):
        eight = pl.ds(8 * k, 8)
        pairs += [(ref.at[eight], land.at[eight]) for ref, land in ((ycol, yc), (acol_hi, ah), (acol_lo, al))]
        pairs.append((stored.at[:, k, :], s.at[k]))
    loads = [pltpu.make_async_copy(source, land, load_sem.at[index]) for index, (source, land) in enumerate(pairs)]
    for load in loads:
        load.start()
    for load in loads[:heads]:
        load.wait()

    @pl.when(jnp.max(size[...]) > 1e-6)
    def _():
        scaled[...], left, right = scale(gn[0].reshape(K, K))
        bound = jnp.max(jnp.sum(jnp.abs(scaled[...]), 1, keepdims=True))
        inverse[...] = unit_matrix() / bound

        def again(state):
            count, rest = state
            return (count < 64) & (rest > 1e-6)

        def step(state):
            inverse[...], rest = refine(scaled[...], inverse[...])
            return state[0] + 1, rest

        lax.while_loop(again, step, (jnp.int32(0), jnp.float32(1.0)))
        mh[...], ml[...] = mixing(inverse[...] * left * right, gn[1].reshape(K, K))

    mix = mh[...], ml[...]
    yr_halves = split(yr[...].reshape(TILE, K))
    row_halves = [ref[...].reshape(TILE, K) for ref in (rh, rl)]
    wrow = split(dot3([jnp.concatenate(pair, 1) for pair in zip(yr_halves, row_halves)], mix))
    left_pair = [jnp.concatenate(pair, 1) for pair in zip(row_halves, wrow)]
    stores = []
    for k in range(SLOTS):
        for load in loads[heads + 4 * k : heads + 4 * k + 4]:
            load.wait()

        @pl.when(8 * k + col == row)
        def _():
            value = s[k]
            down = lax.broadcasted_iota(jnp.int32, (TILE, TILE), 0)
            along = lax.broadcasted_iota(jnp.int32, (TILE, TILE), 1)
            s[k] = jnp.where(down >= along, value, 0.0) + jnp.where(down > along, value, 0.0).T

        @pl.when(8 * k + col > row)
        def _():
            s[k] = jnp.zeros((TILE, TILE), F32)

        @pl.when(8 * k + col <= row)
        def _():
            y_halves = split(yc[8 * k : 8 * k + 8].reshape(TILE, K))
            a_halves = [ref[8 * k : 8 * k + 8].reshape(TILE, K) for ref in (ah, al)]
            wcol = split(dot3([jnp.concatenate(pair, 1) for pair in zip(y_halves, a_halves)], mix))
            right_pair = [jnp.concatenate(pair, 1) for pair in zip(wcol, a_halves)]
            s[k] -= dot3(left_pair, right_pair, NT)

        stores.append(pltpu.make_async_copy(s.at[k], out.at[:, k, :], out_sem.at[k]))
        stores[-1].start()
    for store in stores:
        store.wait()


def body(stored, panel):
    any_spec = pl.BlockSpec(memory_space=pl.ANY)
    vmem, dma = pltpu.VMEM, pltpu.SemaphoreType.DMA
    col_shape, row_shape, square, wide = (32, CHUNK, K), (8, CHUNK, K), (16, 2, 8, K), (2 * K, K)
    out_types = [(col_shape, BF16)] * 2 + [(row_shape, BF16)] * 2 + [(col_shape, F32), (row_shape, F32)]
    out_types += [(square, F32)] * 2 + [(wide, BF16)] * 2 + [((8, 128), F32)]
    small = [
        vmem(square, F32),
        vmem((16, 8, K), F32),
        vmem((16, 8, K), F32),
        vmem((2, 16, 8, K), F32),
        vmem(square, F32),
    ]
    parts = pl.pallas_call(
        exchange_kernel,
        out_shape=[jax.ShapeDtypeStruct(shape, kind) for shape, kind in out_types],
        in_specs=[any_spec] * 2,
        out_specs=[any_spec] * len(out_types),
        scratch_shapes=[
            vmem((SLOTS, TILE, TILE), F32),
            vmem((TILE, K // 8), F32),
            vmem((8, 8, 16, 128), F32),
            vmem((8, 16, 128), F32),
            vmem(col_shape, F32),
            vmem(row_shape, F32),
            vmem(col_shape, BF16),
            vmem(col_shape, BF16),
            vmem(row_shape, BF16),
            vmem(row_shape, BF16),
            vmem(row_shape, F32),
            vmem(row_shape, F32),
            vmem(row_shape, F32),
            vmem(row_shape, F32),
            vmem((2, 3, CHUNK, K), F32),
            vmem((2, CHUNK // 2, K), F32),
            vmem(col_shape, F32),
            vmem((16, CHUNK, K), F32),
            vmem((4, 3, CHUNK, K), F32),
            vmem((3, CHUNK, K), F32),
            vmem(col_shape, F32),
            vmem(row_shape, F32),
            *small,
            *small,
            vmem((K, K), F32),
            vmem((K, K), F32),
            vmem(wide, BF16),
            vmem(wide, BF16),
            vmem((8, 128), F32),
            dma((SLOTS + 1,)),
            dma((11,)),
            dma((SENDS,)),
            dma((RECVS,)),
        ],
        compiler_params=pltpu.CompilerParams(collective_id=0, has_side_effects=True, vmem_limit_bytes=56 << 20),
        name="exchange",
    )(stored, panel)
    return pl.pallas_call(
        update_kernel,
        out_shape=jax.ShapeDtypeStruct(stored.shape, F32),
        in_specs=[any_spec] * (1 + len(out_types)),
        out_specs=any_spec,
        scratch_shapes=[
            vmem((SLOTS, TILE, TILE), F32),
            vmem(col_shape, BF16),
            vmem(col_shape, BF16),
            vmem(row_shape, BF16),
            vmem(row_shape, BF16),
            vmem(col_shape, F32),
            vmem(row_shape, F32),
            vmem((2, *square), F32),
            vmem(wide, BF16),
            vmem(wide, BF16),
            vmem((8, 128), F32),
            vmem((K, K), F32),
            vmem((K, K), F32),
            dma((24,)),
            dma((SLOTS,)),
        ],
        compiler_params=pltpu.CompilerParams(vmem_limit_bytes=56 << 20),
        name="update",
    )(stored, *parts)


def solution(mesh):
    in_specs = (P("row", None, "col"), P("row", "col"))
    out_specs = P("row", None, "col")
    return jax.shard_map(body, mesh=mesh, in_specs=in_specs, out_specs=out_specs, check_vma=False)
```

```python
import functools

import jax
import jax.numpy as jnp
from jax import lax
from jax.experimental import pallas as pl
from jax.experimental.pallas import tpu as pltpu
from jax.sharding import PartitionSpec as P

F32 = jnp.float32
BF16 = jnp.bfloat16
HIGHEST = lax.Precision.HIGHEST
MESH = pl.DeviceIdType.MESH
TILE = 512
K = 256
SLOTS = 4
SENDS, RECVS = 22, 54
CHUNK = 64
NN = (((1,), (0,)), ((), ()))
NT = (((1,), (1,)), ((), ()))


def split(value):
    high = value.astype(BF16)
    return high, (value - high.astype(F32)).astype(BF16)


def dot3(left, right, dims=NN):
    (lh, ll), (rh, rl) = left, right
    dot = functools.partial(lax.dot_general, dimension_numbers=dims, preferred_element_type=F32)
    return dot(lh, rh) + (dot(lh, rl) + dot(ll, rh))


def dot6(left, right, dims=NN):
    return lax.dot_general(left, right, dims, precision=HIGHEST, preferred_element_type=F32)


def mod(value, size):
    return lax.rem(value, size)


class Place:
    def __init__(self):
        self.row = lax.axis_index("row")
        self.col = lax.axis_index("col")
        self.x = lax.div(self.row, 8)
        self.inner = mod(self.row, 8)
        self.y = lax.div(self.inner, 2)
        self.core = mod(self.row, 2)
        self.u = self.y * (1 - self.core) + self.x * self.core
        self.v = self.x * (1 - self.core) + self.y * self.core

    def ring(self, du, dv):
        u, v = mod(self.u + du, 4), mod(self.v + dv, 4)
        return (8 * v + 2 * u) * (1 - self.core) + (8 * u + 2 * v + 1) * self.core

    def at(self, du, dv):
        return {"row": self.ring(du, dv), "col": self.col}

    def sibling(self):
        return {"row": self.row + 1 - 2 * self.core, "col": self.col}

    def up(self, dz):
        return {"row": self.row, "col": mod(self.col + dz % 8, 8)}


class Links:
    def __init__(self, send, recv):
        self.send, self.recv = send, recv
        self.sends, self.slots = 0, 0
        self.ends = []

    def slot(self):
        self.slots += 1
        return self.slots - 1

    def batch(self, ref, when=None):
        self.sends += 1
        self.ends.append((self.sends - 1, ref, when))
        return self.sends - 1

    def copy(self, source, target, slot, device, send):
        return pltpu.make_async_remote_copy(
            src_ref=source,
            dst_ref=target,
            send_sem=self.send.at[send],
            recv_sem=self.recv.at[slot],
            device_id=device,
            device_id_type=MESH,
        )

    def start(self, source, target, slot, device, send=None, when=None):
        send = self.batch(source) if send is None else send
        copy = self.copy(source, target, slot, device, send)
        copy.start() if when is None else pl.when(when)(copy.start)

    def wait(self, ref, slot, device, when=None):
        copy = self.copy(ref, ref, slot, device, 0)
        copy.wait_recv() if when is None else pl.when(when)(copy.wait_recv)

    def finish(self, device):
        for send, ref, when in self.ends:
            copy = self.copy(ref, ref, 0, device, send)
            copy.wait_send() if when is None else pl.when(when)(copy.wait_send)


def plane_gather(place, links, buf):
    near = [None] + [links.slot() for _ in range(3)]
    far = [links.slot() for _ in range(4)]
    across = links.slot()
    batch = links.batch(buf.at[pl.ds(0, 31)])

    def send(du, dv, slot, device):
        ref = buf.at[place.ring(du, dv)]
        links.start(ref, ref, slot, device, batch)

    def spread(du):
        for way in (2, 1, 3):
            send(du, 0, far[du], place.at(0, way))
        send(du, 0, across, place.sibling())

    for way in (2, 1, 3):
        send(0, 0, near[way], place.at(way, 0))
    spread(0)
    yield
    for way in (1, 3, 2):
        links.wait(buf.at[place.ring(4 - way, 0)], near[way], place.at(4 - way, 0))
        spread(4 - way)
        yield
    for du in (0, 3, 1, 2):
        links.wait(buf.at[pl.ds(0, 3)], far[du], place.at(0, 1))
        for way in (1, 3, 2):
            send(du, way, across, place.sibling())
        yield
    links.wait(buf.at[pl.ds(0, 16)], across, place.sibling())


def plane_sum(place, links, buf, sib, vland, uland):
    sib_slots = [links.slot() for _ in range(SLOTS)]
    vs = [links.slot() for _ in range(4)]
    us = links.slot()
    batch = links.batch(buf.at[pl.ds(0, 31)])
    for tile in range(SLOTS):
        for y in range(4):
            links.start(
                buf.at[8 * tile + 2 * y + 1 - place.core],
                sib.at[4 * tile + y],
                sib_slots[tile],
                place.sibling(),
                batch,
            )
        yield
    for tile in range(SLOTS):
        links.wait(sib.at[pl.ds(4 * tile, 4)], sib_slots[tile], place.sibling())
        for y in range(4):
            buf[8 * tile + 2 * y + place.core] += sib[4 * tile + y]
    order = (2, 1, 3, 0)
    for core in range(2):
        for du in order:
            for way in (2, 1, 3):
                links.start(
                    buf.at[place.ring(du, way)],
                    vland.at[du, way - 1],
                    vs[du],
                    place.at(0, way),
                    batch,
                    place.core == core,
                )
        yield
    for du in order:
        links.wait(vland.at[du], vs[du], place.at(0, 1))
        chunk = place.ring(du, 0)
        buf[chunk] += vland[du, 0] + (vland[du, 1] + vland[du, 2])
        if du:
            links.start(buf.at[chunk], uland.at[du - 1], us, place.at(du, 0), batch)
        yield
    links.wait(uland, us, place.at(1, 0))
    buf[place.ring(0, 0)] += uland[0] + (uland[1] + uland[2])


def small_sum(place, links, value, sib, chips, depth, total):
    chip = lax.div(place.row, 2)
    sib_slot, chip_slot, depth_slot, back_slot, last_slot = [links.slot() for _ in range(5)]

    def peer(step):
        index = mod(chip + step, 16)
        return index, {"row": 2 * index + place.core, "col": place.col}

    links.start(value.at[:, 1 - place.core], sib, sib_slot, place.sibling())
    yield
    links.wait(sib, sib_slot, place.sibling())
    for index in range(16):
        chips[index] = value[index, place.core] + sib[index]
    batch = links.batch(chips.at[pl.ds(0, 15)])
    for step in range(1, 16):
        index, device = peer(step)
        links.start(chips.at[index], depth.at[0, chip], chip_slot, device, batch)
    yield
    links.wait(depth.at[0, pl.ds(0, 15)], chip_slot, place.sibling())
    depth[0, chip] = chips[chip]
    depth[1, place.col] = jnp.sum(depth[0], 0)
    batch = links.batch(depth.at[1, pl.ds(0, 7)])
    for step in range(1, 8):
        links.start(depth.at[1, place.col], depth.at[1, place.col], depth_slot, place.up(step), batch)
    yield
    links.wait(depth.at[1, pl.ds(0, 7)], depth_slot, place.up(1))
    total[chip, place.core] = jnp.sum(depth[1, :8], 0)
    own = total.at[chip, place.core]
    batch = links.batch(total.at[pl.ds(0, 15), place.core])
    for step in range(1, 16):
        links.start(own, own, back_slot, peer(step)[1], batch)
    yield
    links.wait(total.at[pl.ds(0, 15), place.core], back_slot, place.sibling())
    links.start(total.at[:, place.core], total.at[:, place.core], last_slot, place.sibling())
    yield
    links.wait(total.at[:, 1 - place.core], last_slot, place.sibling())


def ring_gather(place, links, buf):
    rows = buf.shape[1]
    part = (pl.ds(0, rows // 2), pl.ds(rows // 2, rows // 2))
    one, two, three, four = [(links.slot(), links.slot()) for _ in range(4)]
    wholes, halves = links.batch(buf.at[pl.ds(0, 6)]), links.batch(buf.at[0])
    ways = ((0, 1), (1, -1))

    def piece(offset):
        return buf.at[mod(place.col + offset % 8, 8)]

    def half(offset, which):
        return buf.at[mod(place.col + offset % 8, 8), part[which]]

    for which, way in ways:
        links.start(piece(0), piece(0), two[which], place.up(2 * way), wholes)
    for which, way in ways:
        links.start(piece(0), piece(0), one[which], place.up(way), wholes)
    yield
    for which, way in ways:
        source = piece(-2 * way)
        links.wait(source, two[which], place.up(-2 * way))
        links.start(half(-2 * way, which), half(-2 * way, which), four[which], place.up(2 * way), halves)
        links.start(source, source, three[which], place.up(way), wholes)
    yield
    for which, way in ways:
        links.wait(piece(-way), one[which], place.up(-way))
        links.wait(piece(-3 * way), three[which], place.up(-way))
        links.wait(half(-4 * way, which), four[which], place.up(-2 * way))


def ring_sum(place, links, buf, land, half_land):
    rows = buf.shape[1]
    part = (pl.ds(0, rows // 2), pl.ds(rows // 2, rows // 2))
    one, two, three, four = [(links.slot(), links.slot()) for _ in range(4)]
    wholes, halves = links.batch(buf.at[pl.ds(0, 6)]), links.batch(buf.at[0])
    ways = ((0, 1), (1, -1))

    def piece(offset):
        return mod(place.col + offset % 8, 8)

    for which, way in ways:
        links.start(buf.at[piece(4 * way), part[which]], half_land.at[which], four[which], place.up(2 * way), halves)
        links.start(buf.at[piece(3 * way)], land.at[which, 2], three[which], place.up(way), wholes)
    for which, way in ways:
        links.start(buf.at[piece(way)], land.at[which, 0], one[which], place.up(way), wholes)
    yield
    for which, way in ways:
        links.wait(land.at[which, 2], three[which], place.up(-way))
        links.wait(half_land.at[which], four[which], place.up(-2 * way))
        index = piece(2 * way)
        buf[index] += land[which, 2]
        buf[index, part[which]] += half_land[which]
        links.start(buf.at[index], land.at[which, 1], two[which], place.up(2 * way), wholes)
    yield
    for which, way in ways:
        links.wait(land.at[which, 0], one[which], place.up(-way))
        links.wait(land.at[which, 1], two[which], place.up(-2 * way))
    buf[place.col] += (land[0, 0] + land[1, 0]) + (land[0, 1] + land[1, 1])


class Group:
    def __init__(self, place, links, source, target):
        self.place, self.links, self.source, self.target = place, links, source, target
        self.slot = links.slot()
        self.batch = links.batch(target.at[pl.ds(0, 7)])

    def send(self, index):
        place = self.place
        here = place.inner == index

        @pl.when(here)
        def _():
            self.target[place.inner] = self.source[index]

        device = {"row": place.row - place.inner + index, "col": place.col}
        self.links.start(
            self.source.at[index], self.target.at[place.inner], self.slot, device, self.batch, jnp.logical_not(here)
        )

    def wait(self):
        self.links.wait(self.target.at[pl.ds(0, 7)], self.slot, self.place.sibling())


class Turn:
    def __init__(self, place, links, target, own, other):
        self.place, self.links, self.target, self.own, self.other = place, links, target, own, other
        self.slot = links.slot()
        self.batches = links.batch(target.at[pl.ds(0, 7)], own), links.batch(target.at[pl.ds(0, 8)], other)

    def start(self, source, target, device, when):
        for batch, side in zip(self.batches, (self.own, self.other)):
            if when is None:
                self.links.start(source, target, self.slot, device, batch, side)
            elif side is self.other:
                self.links.start(source, target, self.slot, device, batch, side)

    def wait(self):
        self.links.wait(self.target.at[pl.ds(0, 7)], self.slot, self.place.sibling(), self.own)
        self.links.wait(self.target.at[pl.ds(0, 8)], self.slot, self.place.sibling(), self.other)


def unit_matrix():
    return jnp.where(
        lax.broadcasted_iota(jnp.int32, (K, K), 0) == lax.broadcasted_iota(jnp.int32, (K, K), 1), 1.0, 0.0
    ).astype(F32)


def scale(gram):
    diagonal = gram * unit_matrix()
    left = lax.rsqrt(jnp.sum(diagonal, 1, keepdims=True))
    right = lax.rsqrt(jnp.sum(diagonal, 0, keepdims=True))
    return gram * left * right, left, right


def refine(scaled, inverse):
    rest = unit_matrix() - dot6(scaled, inverse)
    return inverse + dot3(split(inverse), split(rest)), jnp.sum(rest * rest)


def mixing(inverse, lower):
    halves = split(inverse)
    twist = dot3(halves, split(dot3(split(lower + lower.T), halves)))
    return split(jnp.concatenate([2.0 * inverse, -2.0 * twist], 0))


def pack(slab, pieces):
    low = lax.broadcasted_iota(jnp.int32, (16, 128), 1) < CHUNK
    for pair in range(4):
        first, second = [slab[16 * side : 16 * side + 16, 128 * pair : 128 * pair + 128] for side in range(2)]
        pieces[2 * pair] = jnp.where(low, first, pltpu.roll(second, CHUNK, 1))
        pieces[2 * pair + 1] = jnp.where(low, pltpu.roll(first, CHUNK, 1), second)


def unpack(pieces):
    turned = pieces.reshape(128, 128).T
    return jnp.concatenate([turned[:CHUNK], turned[CHUNK:]], 1)


def unpack_row(slabs):
    return jnp.concatenate([slabs[index, 16 * side : 16 * side + 16, :] for side in range(2) for index in range(8)], 0)


def exchange_kernel(
    stored,
    panel,
    acol_hi_out,
    acol_lo_out,
    arow_hi_out,
    arow_lo_out,
    ycol_out,
    yrow_out,
    gram_out,
    lower_out,
    mix_hi_out,
    mix_lo_out,
    size_out,
    s,
    slabs,
    packed,
    colpk,
    acol,
    turned,
    acol_hi,
    acol_lo,
    arow_hi,
    arow_lo,
    rows,
    diag,
    whole,
    swapped,
    zland,
    zhalf,
    part,
    sib,
    vland,
    uland,
    ycol,
    yrow,
    gvalue,
    gsib,
    gchips,
    gdepth,
    gtotal,
    nvalue,
    nsib,
    nchips,
    ndepth,
    ntotal,
    scaled,
    inverse,
    mix_hi,
    mix_lo,
    size,
    load_sem,
    out_sem,
    send_sem,
    recv_sem,
):
    place = Place()
    links = Links(send_sem, recv_sem)
    row, col, inner = place.row, place.col, place.inner
    base = row - inner
    fetch = pltpu.make_async_copy(panel, slabs.at[col], load_sem.at[SLOTS])
    fetch.start()
    loads = [pltpu.make_async_copy(stored.at[:, k, :], s.at[k], load_sem.at[k]) for k in range(SLOTS)]
    for load in loads:
        load.start()

    barrier = pltpu.get_barrier_semaphore()

    def greet(device):
        pl.semaphore_signal(barrier, inc=1, device_id=device, device_id_type=MESH)

    own = inner == col
    other = jnp.logical_not(own)
    for step in range(1, 8):
        greet({"row": base + mod(inner + step, 8), "col": inner})
        greet({"row": base + col, "col": mod(col + step, 8)})
        greet(place.up(step))
        greet({"row": base + mod(inner + step, 8), "col": col})
    for step in range(1, 16):
        greet({"row": mod(row + 2 * step, 32), "col": col})

    @pl.when(other)
    def _():
        greet({"row": row, "col": inner})
        greet({"row": base + col, "col": col})

    fetch.wait()
    pack(slabs[col], packed)
    pl.when(own)(lambda: pl.semaphore_wait(barrier, 43))
    pl.when(other)(lambda: pl.semaphore_wait(barrier, 45))

    turn = Turn(place, links, colpk, own, other)
    for step in range(8):
        piece = mod(inner + step, 8)
        device = {"row": base + piece, "col": inner}
        turn.start(packed.at[piece], colpk.at[col], device, None if step else other)
    deep = ring_gather(place, links, slabs)
    next(deep)

    @pl.when(own)
    def _():
        colpk[col] = packed[inner]

    for load in loads:
        load.wait()

    @pl.when(own)
    def _():
        value = s[place.x]
        below = lax.broadcasted_iota(jnp.int32, (TILE, TILE), 0)
        across = lax.broadcasted_iota(jnp.int32, (TILE, TILE), 1)
        s[place.x] = jnp.where(below >= across, value, 0.0) + jnp.where(below > across, value, 0.0).T

    next(deep)
    turn.wait()
    acol[row] = unpack(colpk[...])
    wide = plane_gather(place, links, acol)
    next(wide)
    chunk = acol[row]
    gvalue[...] = dot6(chunk.T, chunk).reshape(gvalue.shape)
    gsum = small_sum(place, links, gvalue, gsib, gchips, gdepth, gtotal)
    next(gsum)
    for _ in deep:
        pass
    for _ in range(3):
        next(wide)

    def store_halves(source, high, low, outs, sems):
        high[...], low[...] = split(source)
        copies = [pltpu.make_async_copy(ref, out, out_sem.at[sem]) for ref, out, sem in zip((high, low), outs, sems)]
        for copy in copies:
            copy.start()
        return copies

    turned[...] = unpack_row(slabs[...])
    copies = store_halves(turned[...].T.reshape(8, CHUNK, K), arow_hi, arow_lo, (arow_hi_out, arow_lo_out), (0, 1))
    next(gsum)
    next(wide)

    tall = plane_sum(place, links, part, sib, vland, uland)
    for k in range(SLOTS):
        part[8 * k : 8 * k + 8] = jnp.zeros((8, CHUNK, K), F32)

        @pl.when(8 * k + col < row)
        def _():
            terms = dot3(split(s[k].T), [ref[...].reshape(TILE, K) for ref in (arow_hi, arow_lo)])
            part[8 * k : 8 * k + 8] = terms.reshape(8, CHUNK, K)

        next(tall)
        if k < 3:
            next(wide)
    next(tall)
    next(gsum)
    for _ in wide:
        pass
    copies += store_halves(acol[...], acol_hi, acol_lo, (acol_hi_out, acol_lo_out), (2, 3))

    rows[...] = jnp.zeros_like(rows)
    diag[...] = jnp.zeros_like(diag)
    group = Group(place, links, whole, swapped)
    for block in range(2):
        chunks = pl.ds(4 * block, 4)
        span = pl.ds(TILE // 2 * block, TILE // 2)

        def row_terms(k, carry):
            @pl.when(8 * k + col < row)
            def _():
                right = [ref[pl.ds(8 * k, 8)].reshape(TILE, K) for ref in (acol_hi, acol_lo)]
                rows[chunks] += dot3(split(s[k, span]), right).reshape(4, CHUNK, K)

            return carry

        lax.fori_loop(0, SLOTS, row_terms, 0)

        @pl.when(own)
        def _():
            right = [ref[...].reshape(TILE, K) for ref in (arow_hi, arow_lo)]
            diag[chunks] = dot3(split(s[place.x, span]), right).reshape(4, CHUNK, K)

        whole[chunks] = rows[chunks] + diag[chunks]
        for index in range(4 * block, 4 * block + 4):
            group.send(index)

    terms = (rows[...] + 0.5 * diag[...]).reshape(TILE, K)
    lower = dot3(split(turned[...]), split(terms))
    nvalue[...] = lower.reshape(nvalue.shape)
    nsum = small_sum(place, links, nvalue, nsib, nchips, ndepth, ntotal)
    next(nsum)
    next(tall)
    next(gsum)
    next(nsum)
    group.wait()
    deep = ring_sum(place, links, swapped, zland, zhalf)
    next(deep)
    next(gsum)
    next(deep)
    next(nsum)
    for _ in range(4):
        next(tall)
    for _ in gsum:
        pass
    scaled[...], left, right = scale(gtotal[...].reshape(K, K))
    rest = unit_matrix() - scaled[...]
    square = dot3(split(rest), split(rest))
    close = jnp.sum(square * square) < 0.8
    bound = jnp.max(jnp.sum(jnp.abs(scaled[...]), 1, keepdims=True))
    inverse[...] = jnp.where(close, unit_matrix() + rest, unit_matrix() / bound)
    for _ in deep:
        pass
    for _ in tall:
        pass
    product = part[row] + swapped[col]
    ycol[row] = product

    wide = plane_gather(place, links, ycol)
    next(wide)
    turn = Turn(place, links, yrow, own, other)
    for step in range(8):
        piece = mod(col + step, 8)
        device = {"row": base + col, "col": piece}
        turn.start(ycol.at[row], yrow.at[inner], device, None if step else other)

    @pl.when(own)
    def _():
        yrow[inner] = product

    next(nsum)
    inverse[...], _ = refine(scaled[...], inverse[...])
    for _ in range(3):
        next(wide)
    next(nsum)
    inverse[...], _ = refine(scaled[...], inverse[...])
    next(wide)
    inverse[...], _ = refine(scaled[...], inverse[...])
    next(wide)
    inverse[...], final = refine(scaled[...], inverse[...])
    size[...] = jnp.full(size.shape, final, F32)
    next(wide)

    def keep(ref, out, sem):
        copies.append(pltpu.make_async_copy(ref, out, out_sem.at[sem]))
        copies[-1].start()

    def keep_cols(core, sem):
        for chip in range(16):
            chunk = 2 * chip + core
            pltpu.make_async_copy(ycol.at[chunk], ycol_out.at[chunk], out_sem.at[sem]).start()
        copies.append(pltpu.make_async_copy(ycol.at[pl.ds(0, 16)], ycol_out.at[pl.ds(0, 16)], out_sem.at[sem]))

    for _ in nsum:
        pass
    mix_hi[...], mix_lo[...] = mixing(inverse[...] * left * right, ntotal[...].reshape(K, K))
    ends = ((gtotal, gram_out), (ntotal, lower_out), (mix_hi, mix_hi_out), (mix_lo, mix_lo_out), (size, size_out))
    for index, (ref, out) in enumerate(ends):
        keep(ref, out, 4 + index)
    next(wide)
    keep_cols(place.core, 9)
    turn.wait()
    keep(yrow, yrow_out, 10)
    for _ in wide:
        pass
    keep_cols(1 - place.core, 11)
    for copy in copies:
        copy.wait()
    links.finish(place.sibling())


def update_kernel(
    stored,
    acol_hi,
    acol_lo,
    arow_hi,
    arow_lo,
    ycol,
    yrow,
    gram_in,
    lower_in,
    mix_hi,
    mix_lo,
    size_in,
    out,
    s,
    ah,
    al,
    rh,
    rl,
    yc,
    yr,
    gn,
    mh,
    ml,
    size,
    scaled,
    inverse,
    load_sem,
    out_sem,
):
    row, col = lax.axis_index("row"), lax.axis_index("col")
    pairs = [(size_in, size), (mix_hi, mh), (mix_lo, ml), (yrow, yr), (arow_hi, rh), (arow_lo, rl)]
    heads = len(pairs)
    for k in range(SLOTS):
        eight = pl.ds(8 * k, 8)
        pairs += [(ref.at[eight], land.at[eight]) for ref, land in ((ycol, yc), (acol_hi, ah), (acol_lo, al))]
        pairs.append((stored.at[:, k, :], s.at[k]))
    loads = [pltpu.make_async_copy(source, land, load_sem.at[index]) for index, (source, land) in enumerate(pairs)]
    ahead = heads + 4
    for load in loads[:ahead]:
        load.start()
    for load in loads[:heads]:
        load.wait()
    for load in loads[ahead : ahead + 4]:
        load.start()

    @pl.when(jnp.max(size[...]) > 1e-6)
    def _():
        for index, source in enumerate((gram_in, lower_in)):
            load = pltpu.make_async_copy(source, gn.at[index], out_sem.at[index])
            load.start()
            load.wait()
        scaled[...], left, right = scale(gn[0].reshape(K, K))
        bound = jnp.max(jnp.sum(jnp.abs(scaled[...]), 1, keepdims=True))
        inverse[...] = unit_matrix() / bound

        def again(state):
            count, rest = state
            return (count < 64) & (rest > 1e-6)

        def step(state):
            inverse[...], rest = refine(scaled[...], inverse[...])
            return state[0] + 1, rest

        lax.while_loop(again, step, (jnp.int32(0), jnp.float32(1.0)))
        mh[...], ml[...] = mixing(inverse[...] * left * right, gn[1].reshape(K, K))

    mix = mh[...], ml[...]
    yr_halves = split(yr[...].reshape(TILE, K))
    row_halves = [ref[...].reshape(TILE, K) for ref in (rh, rl)]
    wrow = split(dot3([jnp.concatenate(pair, 1) for pair in zip(yr_halves, row_halves)], mix))
    left_pair = [jnp.concatenate(pair, 1) for pair in zip(row_halves, wrow)]
    stores = []
    for k in range(SLOTS):
        for load in loads[heads + 4 * k : heads + 4 * k + 4]:
            load.wait()
        for load in loads[ahead + 4 * k + 4 : ahead + 4 * k + 8]:
            load.start()

        @pl.when(8 * k + col == row)
        def _():
            value = s[k]
            down = lax.broadcasted_iota(jnp.int32, (TILE, TILE), 0)
            along = lax.broadcasted_iota(jnp.int32, (TILE, TILE), 1)
            s[k] = jnp.where(down >= along, value, 0.0) + jnp.where(down > along, value, 0.0).T

        @pl.when(8 * k + col > row)
        def _():
            s[k] = jnp.zeros((TILE, TILE), F32)

        @pl.when(8 * k + col <= row)
        def _():
            y_halves = split(yc[8 * k : 8 * k + 8].reshape(TILE, K))
            a_halves = [ref[8 * k : 8 * k + 8].reshape(TILE, K) for ref in (ah, al)]
            wcol = split(dot3([jnp.concatenate(pair, 1) for pair in zip(y_halves, a_halves)], mix))
            right_pair = [jnp.concatenate(pair, 1) for pair in zip(wcol, a_halves)]
            s[k] -= dot3(left_pair, right_pair, NT)

        stores.append(pltpu.make_async_copy(s.at[k], out.at[:, k, :], out_sem.at[k]))
        stores[-1].start()
    for store in stores:
        store.wait()


def body(stored, panel):
    any_spec = pl.BlockSpec(memory_space=pl.ANY)
    vmem, dma = pltpu.VMEM, pltpu.SemaphoreType.DMA
    col_shape, row_shape, square, wide = (32, CHUNK, K), (8, CHUNK, K), (16, 2, 8, K), (2 * K, K)
    out_types = [(col_shape, BF16)] * 2 + [(row_shape, BF16)] * 2 + [(col_shape, F32), (row_shape, F32)]
    out_types += [(square, F32)] * 2 + [(wide, BF16)] * 2 + [((8, 128), F32)]
    small = [
        vmem(square, F32),
        vmem((16, 8, K), F32),
        vmem((16, 8, K), F32),
        vmem((2, 16, 8, K), F32),
        vmem(square, F32),
    ]
    parts = pl.pallas_call(
        exchange_kernel,
        out_shape=[jax.ShapeDtypeStruct(shape, kind) for shape, kind in out_types],
        in_specs=[any_spec] * 2,
        out_specs=[any_spec] * len(out_types),
        scratch_shapes=[
            vmem((SLOTS, TILE, TILE), F32),
            vmem((8, K // 8, TILE), F32),
            vmem((8, 16, 128), F32),
            vmem((8, 16, 128), F32),
            vmem(col_shape, F32),
            vmem((K, TILE), F32),
            vmem(col_shape, BF16),
            vmem(col_shape, BF16),
            vmem(row_shape, BF16),
            vmem(row_shape, BF16),
            vmem(row_shape, F32),
            vmem(row_shape, F32),
            vmem(row_shape, F32),
            vmem(row_shape, F32),
            vmem((2, 3, CHUNK, K), F32),
            vmem((2, CHUNK // 2, K), F32),
            vmem(col_shape, F32),
            vmem((16, CHUNK, K), F32),
            vmem((4, 3, CHUNK, K), F32),
            vmem((3, CHUNK, K), F32),
            vmem(col_shape, F32),
            vmem(row_shape, F32),
            *small,
            *small,
            vmem((K, K), F32),
            vmem((K, K), F32),
            vmem(wide, BF16),
            vmem(wide, BF16),
            vmem((8, 128), F32),
            dma((SLOTS + 1,)),
            dma((12,)),
            dma((SENDS,)),
            dma((RECVS,)),
        ],
        compiler_params=pltpu.CompilerParams(collective_id=0, has_side_effects=True, vmem_limit_bytes=56 << 20),
        name="exchange",
    )(stored, panel.T)
    return pl.pallas_call(
        update_kernel,
        out_shape=jax.ShapeDtypeStruct(stored.shape, F32),
        in_specs=[any_spec] * (1 + len(out_types)),
        out_specs=any_spec,
        scratch_shapes=[
            vmem((SLOTS, TILE, TILE), F32),
            vmem(col_shape, BF16),
            vmem(col_shape, BF16),
            vmem(row_shape, BF16),
            vmem(row_shape, BF16),
            vmem(col_shape, F32),
            vmem(row_shape, F32),
            vmem((2, *square), F32),
            vmem(wide, BF16),
            vmem(wide, BF16),
            vmem((8, 128), F32),
            vmem((K, K), F32),
            vmem((K, K), F32),
            dma((22,)),
            dma((SLOTS,)),
        ],
        compiler_params=pltpu.CompilerParams(vmem_limit_bytes=56 << 20),
        name="update",
    )(stored, *parts)


def solution(mesh):
    in_specs = (P("row", None, "col"), P("row", "col"))
    out_specs = P("row", None, "col")
    return jax.shard_map(body, mesh=mesh, in_specs=in_specs, out_specs=out_specs, check_vma=False)
```

```python
import functools

import jax
import jax.numpy as jnp
from jax import lax
from jax.experimental import pallas as pl
from jax.experimental.pallas import tpu as pltpu
from jax.sharding import PartitionSpec as P

F32 = jnp.float32
BF16 = jnp.bfloat16
HIGHEST = lax.Precision.HIGHEST
MESH = pl.DeviceIdType.MESH
TILE = 512
K = 256
SLOTS = 4
SENDS, RECVS = 22, 54
CHUNK = 64
NN = (((1,), (0,)), ((), ()))
NT = (((1,), (1,)), ((), ()))


def split(value):
    high = value.astype(BF16)
    return high, (value - high.astype(F32)).astype(BF16)


def dot3(left, right, dims=NN):
    (lh, ll), (rh, rl) = left, right
    dot = functools.partial(lax.dot_general, dimension_numbers=dims, preferred_element_type=F32)
    return dot(lh, rh) + (dot(lh, rl) + dot(ll, rh))


def dot6(left, right, dims=NN):
    return lax.dot_general(left, right, dims, precision=HIGHEST, preferred_element_type=F32)


def mod(value, size):
    return lax.rem(value, size)


class Place:
    def __init__(self):
        self.row = lax.axis_index("row")
        self.col = lax.axis_index("col")
        self.x = lax.div(self.row, 8)
        self.inner = mod(self.row, 8)
        self.y = lax.div(self.inner, 2)
        self.core = mod(self.row, 2)
        self.u = self.y * (1 - self.core) + self.x * self.core
        self.v = self.x * (1 - self.core) + self.y * self.core

    def ring(self, du, dv):
        u, v = mod(self.u + du, 4), mod(self.v + dv, 4)
        return (8 * v + 2 * u) * (1 - self.core) + (8 * u + 2 * v + 1) * self.core

    def at(self, du, dv):
        return {"row": self.ring(du, dv), "col": self.col}

    def sibling(self):
        return {"row": self.row + 1 - 2 * self.core, "col": self.col}

    def up(self, dz):
        return {"row": self.row, "col": mod(self.col + dz % 8, 8)}


class Links:
    def __init__(self, send, recv):
        self.send, self.recv = send, recv
        self.sends, self.slots = 0, 0
        self.ends = []

    def slot(self):
        self.slots += 1
        return self.slots - 1

    def batch(self, ref, when=None):
        self.sends += 1
        self.ends.append((self.sends - 1, ref, when))
        return self.sends - 1

    def copy(self, source, target, slot, device, send):
        return pltpu.make_async_remote_copy(
            src_ref=source,
            dst_ref=target,
            send_sem=self.send.at[send],
            recv_sem=self.recv.at[slot],
            device_id=device,
            device_id_type=MESH,
        )

    def start(self, source, target, slot, device, send=None, when=None):
        send = self.batch(source) if send is None else send
        copy = self.copy(source, target, slot, device, send)
        copy.start() if when is None else pl.when(when)(copy.start)

    def wait(self, ref, slot, device, when=None):
        copy = self.copy(ref, ref, slot, device, 0)
        copy.wait_recv() if when is None else pl.when(when)(copy.wait_recv)

    def finish(self, device):
        for send, ref, when in self.ends:
            copy = self.copy(ref, ref, 0, device, send)
            copy.wait_send() if when is None else pl.when(when)(copy.wait_send)


def plane_gather(place, links, buf, kept=None):
    kept = buf if kept is None else kept
    near = [None] + [links.slot() for _ in range(3)]
    far = [links.slot() for _ in range(4)]
    across = links.slot()
    batch = links.batch(buf.at[pl.ds(0, 31)])

    def send(du, dv, slot, device):
        ref = buf.at[place.ring(du, dv)]
        links.start(ref, ref, slot, device, batch)

    def hand_over(du, dv):
        chunk = place.ring(du, dv)
        links.start(buf.at[chunk], kept.at[chunk], across, place.sibling(), batch)

    def spread(du):
        for way in (2, 1, 3):
            send(du, 0, far[du], place.at(0, way))
        hand_over(du, 0)

    for way in (2, 1, 3):
        send(0, 0, near[way], place.at(way, 0))
    spread(0)
    yield
    for way in (1, 3, 2):
        links.wait(buf.at[place.ring(4 - way, 0)], near[way], place.at(4 - way, 0))
        spread(4 - way)
        yield
    for du in (0, 3, 1, 2):
        links.wait(buf.at[pl.ds(0, 3)], far[du], place.at(0, 1))
        for way in (1, 3, 2):
            hand_over(du, way)
        yield
    links.wait(kept.at[pl.ds(0, 16)], across, place.sibling())


def plane_sum(place, links, buf, sib, vland, uland):
    sib_slots = [links.slot() for _ in range(SLOTS)]
    vs = [links.slot() for _ in range(4)]
    us = links.slot()
    batch = links.batch(buf.at[pl.ds(0, 31)])
    for tile in range(SLOTS):
        for y in range(4):
            links.start(
                buf.at[8 * tile + 2 * y + 1 - place.core],
                sib.at[4 * tile + y],
                sib_slots[tile],
                place.sibling(),
                batch,
            )
        yield
    for tile in range(SLOTS):
        links.wait(sib.at[pl.ds(4 * tile, 4)], sib_slots[tile], place.sibling())
        for y in range(4):
            buf[8 * tile + 2 * y + place.core] += sib[4 * tile + y]
    order = (2, 1, 3, 0)
    for core in range(2):
        for du in order:
            for way in (2, 1, 3):
                links.start(
                    buf.at[place.ring(du, way)],
                    vland.at[du, way - 1],
                    vs[du],
                    place.at(0, way),
                    batch,
                    place.core == core,
                )
        yield
    for du in order:
        links.wait(vland.at[du], vs[du], place.at(0, 1))
        chunk = place.ring(du, 0)
        buf[chunk] += vland[du, 0] + (vland[du, 1] + vland[du, 2])
        if du:
            links.start(buf.at[chunk], uland.at[du - 1], us, place.at(du, 0), batch)
        yield
    links.wait(uland, us, place.at(1, 0))
    buf[place.ring(0, 0)] += uland[0] + (uland[1] + uland[2])


def small_sum(place, links, value, sib, chips, depth, total):
    chip = lax.div(place.row, 2)
    sib_slot, chip_slot, depth_slot, back_slot, last_slot = [links.slot() for _ in range(5)]

    def peer(step):
        index = mod(chip + step, 16)
        return index, {"row": 2 * index + place.core, "col": place.col}

    links.start(value.at[:, 1 - place.core], sib, sib_slot, place.sibling())
    yield
    links.wait(sib, sib_slot, place.sibling())
    for index in range(16):
        chips[index] = value[index, place.core] + sib[index]
    batch = links.batch(chips.at[pl.ds(0, 15)])
    for step in range(1, 16):
        index, device = peer(step)
        links.start(chips.at[index], depth.at[0, chip], chip_slot, device, batch)
    yield
    links.wait(depth.at[0, pl.ds(0, 15)], chip_slot, place.sibling())
    depth[0, chip] = chips[chip]
    depth[1, place.col] = jnp.sum(depth[0], 0)
    batch = links.batch(depth.at[1, pl.ds(0, 7)])
    for step in range(1, 8):
        links.start(depth.at[1, place.col], depth.at[1, place.col], depth_slot, place.up(step), batch)
    yield
    links.wait(depth.at[1, pl.ds(0, 7)], depth_slot, place.up(1))
    total[chip, place.core] = jnp.sum(depth[1, :8], 0)
    own = total.at[chip, place.core]
    batch = links.batch(total.at[pl.ds(0, 15), place.core])
    for step in range(1, 16):
        links.start(own, own, back_slot, peer(step)[1], batch)
    yield
    links.wait(total.at[pl.ds(0, 15), place.core], back_slot, place.sibling())
    links.start(total.at[:, place.core], total.at[:, place.core], last_slot, place.sibling())
    yield
    links.wait(total.at[:, 1 - place.core], last_slot, place.sibling())


def ring_gather(place, links, buf):
    rows = buf.shape[1]
    part = (pl.ds(0, rows // 2), pl.ds(rows // 2, rows // 2))
    one, two, three, four = [(links.slot(), links.slot()) for _ in range(4)]
    wholes, halves = links.batch(buf.at[pl.ds(0, 6)]), links.batch(buf.at[0])
    ways = ((0, 1), (1, -1))

    def piece(offset):
        return buf.at[mod(place.col + offset % 8, 8)]

    def half(offset, which):
        return buf.at[mod(place.col + offset % 8, 8), part[which]]

    for which, way in ways:
        links.start(piece(0), piece(0), two[which], place.up(2 * way), wholes)
    for which, way in ways:
        links.start(piece(0), piece(0), one[which], place.up(way), wholes)
    yield
    for which, way in ways:
        source = piece(-2 * way)
        links.wait(source, two[which], place.up(-2 * way))
        links.start(half(-2 * way, which), half(-2 * way, which), four[which], place.up(2 * way), halves)
        links.start(source, source, three[which], place.up(way), wholes)
    yield
    for which, way in ways:
        links.wait(piece(-way), one[which], place.up(-way))
        links.wait(piece(-3 * way), three[which], place.up(-way))
        links.wait(half(-4 * way, which), four[which], place.up(-2 * way))


def ring_sum(place, links, buf, land, half_land):
    rows = buf.shape[1]
    part = (pl.ds(0, rows // 2), pl.ds(rows // 2, rows // 2))
    one, two, three, four = [(links.slot(), links.slot()) for _ in range(4)]
    wholes, halves = links.batch(buf.at[pl.ds(0, 6)]), links.batch(buf.at[0])
    ways = ((0, 1), (1, -1))

    def piece(offset):
        return mod(place.col + offset % 8, 8)

    for which, way in ways:
        links.start(buf.at[piece(4 * way), part[which]], half_land.at[which], four[which], place.up(2 * way), halves)
        links.start(buf.at[piece(3 * way)], land.at[which, 2], three[which], place.up(way), wholes)
    for which, way in ways:
        links.start(buf.at[piece(way)], land.at[which, 0], one[which], place.up(way), wholes)
    yield
    for which, way in ways:
        links.wait(land.at[which, 2], three[which], place.up(-way))
        links.wait(half_land.at[which], four[which], place.up(-2 * way))
        index = piece(2 * way)
        buf[index] += land[which, 2]
        buf[index, part[which]] += half_land[which]
        links.start(buf.at[index], land.at[which, 1], two[which], place.up(2 * way), wholes)
    yield
    for which, way in ways:
        links.wait(land.at[which, 0], one[which], place.up(-way))
        links.wait(land.at[which, 1], two[which], place.up(-2 * way))
    buf[place.col] += (land[0, 0] + land[1, 0]) + (land[0, 1] + land[1, 1])


class Group:
    def __init__(self, place, links, source, target):
        self.place, self.links, self.source, self.target = place, links, source, target
        self.slot = links.slot()
        self.batch = links.batch(target.at[pl.ds(0, 7)])

    def send(self, index):
        place = self.place
        here = place.inner == index

        @pl.when(here)
        def _():
            self.target[place.inner] = self.source[index]

        device = {"row": place.row - place.inner + index, "col": place.col}
        self.links.start(
            self.source.at[index], self.target.at[place.inner], self.slot, device, self.batch, jnp.logical_not(here)
        )

    def wait(self):
        self.links.wait(self.target.at[pl.ds(0, 7)], self.slot, self.place.sibling())


class Turn:
    def __init__(self, place, links, target, own, other):
        self.place, self.links, self.target, self.own, self.other = place, links, target, own, other
        self.slot = links.slot()
        self.batches = links.batch(target.at[pl.ds(0, 7)], own), links.batch(target.at[pl.ds(0, 8)], other)

    def start(self, source, target, device, when):
        for batch, side in zip(self.batches, (self.own, self.other)):
            if when is None:
                self.links.start(source, target, self.slot, device, batch, side)
            elif side is self.other:
                self.links.start(source, target, self.slot, device, batch, side)

    def wait(self):
        self.links.wait(self.target.at[pl.ds(0, 7)], self.slot, self.place.sibling(), self.own)
        self.links.wait(self.target.at[pl.ds(0, 8)], self.slot, self.place.sibling(), self.other)


def unit_matrix():
    return jnp.where(
        lax.broadcasted_iota(jnp.int32, (K, K), 0) == lax.broadcasted_iota(jnp.int32, (K, K), 1), 1.0, 0.0
    ).astype(F32)


def scale(gram):
    diagonal = gram * unit_matrix()
    left = lax.rsqrt(jnp.sum(diagonal, 1, keepdims=True))
    right = lax.rsqrt(jnp.sum(diagonal, 0, keepdims=True))
    return gram * left * right, left, right


def refine(scaled, inverse):
    rest = unit_matrix() - dot6(scaled, inverse)
    return inverse + dot3(split(inverse), split(rest)), jnp.sum(rest * rest)


def mixing(inverse, lower):
    halves = split(inverse)
    twist = dot3(halves, split(dot3(split(lower + lower.T), halves)))
    return split(jnp.concatenate([2.0 * inverse, -2.0 * twist], 0))


def pack(slab, pieces):
    low = lax.broadcasted_iota(jnp.int32, (16, 128), 1) < CHUNK
    for pair in range(4):
        first, second = [slab[16 * side : 16 * side + 16, 128 * pair : 128 * pair + 128] for side in range(2)]
        pieces[2 * pair] = jnp.where(low, first, pltpu.roll(second, CHUNK, 1))
        pieces[2 * pair + 1] = jnp.where(low, pltpu.roll(first, CHUNK, 1), second)


def unpack(pieces):
    turned = pieces.reshape(128, 128).T
    return jnp.concatenate([turned[:CHUNK], turned[CHUNK:]], 1)


def unpack_row(slabs):
    return jnp.concatenate([slabs[index, 16 * side : 16 * side + 16, :] for side in range(2) for index in range(8)], 0)


def exchange_kernel(
    stored,
    panel,
    acol_hi_out,
    acol_lo_out,
    arow_hi_out,
    arow_lo_out,
    ycol_out,
    yrow_out,
    gram_out,
    lower_out,
    mix_hi_out,
    mix_lo_out,
    size_out,
    s,
    slabs,
    packed,
    colpk,
    acol,
    turned,
    acol_hi,
    acol_lo,
    arow_hi,
    arow_lo,
    rows,
    diag,
    whole,
    swapped,
    zland,
    zhalf,
    part,
    sib,
    vland,
    uland,
    ycol,
    gvalue,
    gsib,
    gchips,
    gdepth,
    gtotal,
    nvalue,
    nsib,
    nchips,
    ndepth,
    ntotal,
    scaled,
    inverse,
    mix_hi,
    mix_lo,
    size,
    load_sem,
    out_sem,
    send_sem,
    recv_sem,
):
    place = Place()
    links = Links(send_sem, recv_sem)
    row, col, inner = place.row, place.col, place.inner
    base = row - inner
    fetch = pltpu.make_async_copy(panel, slabs.at[col], load_sem.at[SLOTS])
    fetch.start()
    loads = [pltpu.make_async_copy(stored.at[:, k, :], s.at[k], load_sem.at[k]) for k in range(SLOTS)]
    for load in loads:
        load.start()

    barrier = pltpu.get_barrier_semaphore()

    def greet(device):
        pl.semaphore_signal(barrier, inc=1, device_id=device, device_id_type=MESH)

    own = inner == col
    other = jnp.logical_not(own)
    for step in range(1, 8):
        greet({"row": base + mod(inner + step, 8), "col": inner})
        greet({"row": base + col, "col": mod(col + step, 8)})
        greet(place.up(step))
        greet({"row": base + mod(inner + step, 8), "col": col})
    for step in range(1, 16):
        greet({"row": mod(row + 2 * step, 32), "col": col})

    @pl.when(other)
    def _():
        greet({"row": row, "col": inner})
        greet({"row": base + col, "col": col})

    fetch.wait()
    pack(slabs[col], packed)
    pl.when(own)(lambda: pl.semaphore_wait(barrier, 43))
    pl.when(other)(lambda: pl.semaphore_wait(barrier, 45))

    turn = Turn(place, links, colpk, own, other)
    for step in range(8):
        piece = mod(inner + step, 8)
        device = {"row": base + piece, "col": inner}
        turn.start(packed.at[piece], colpk.at[col], device, None if step else other)
    deep = ring_gather(place, links, slabs)
    next(deep)

    @pl.when(own)
    def _():
        colpk[col] = packed[inner]

    for load in loads:
        load.wait()

    @pl.when(own)
    def _():
        value = s[place.x]
        below = lax.broadcasted_iota(jnp.int32, (TILE, TILE), 0)
        across = lax.broadcasted_iota(jnp.int32, (TILE, TILE), 1)
        s[place.x] = jnp.where(below >= across, value, 0.0) + jnp.where(below > across, value, 0.0).T

    next(deep)
    turn.wait()
    acol[row] = unpack(colpk[...])
    wide = plane_gather(place, links, acol)
    next(wide)
    chunk = acol[row]
    gvalue[...] = dot6(chunk.T, chunk).reshape(gvalue.shape)
    gsum = small_sum(place, links, gvalue, gsib, gchips, gdepth, gtotal)
    next(gsum)
    for _ in deep:
        pass
    for _ in range(3):
        next(wide)

    def store_halves(source, high, low, outs, sems):
        high[...], low[...] = split(source)
        copies = [pltpu.make_async_copy(ref, out, out_sem.at[sem]) for ref, out, sem in zip((high, low), outs, sems)]
        for copy in copies:
            copy.start()
        return copies

    turned[...] = unpack_row(slabs[...])
    copies = store_halves(turned[...].T.reshape(8, CHUNK, K), arow_hi, arow_lo, (arow_hi_out, arow_lo_out), (0, 1))
    next(gsum)
    next(wide)

    tall = plane_sum(place, links, part, sib, vland, uland)
    for k in range(SLOTS):
        part[8 * k : 8 * k + 8] = jnp.zeros((8, CHUNK, K), F32)

        @pl.when(8 * k + col < row)
        def _():
            terms = dot3(split(s[k].T), [ref[...].reshape(TILE, K) for ref in (arow_hi, arow_lo)])
            part[8 * k : 8 * k + 8] = terms.reshape(8, CHUNK, K)

        next(tall)
        if k < 3:
            next(wide)
    next(tall)
    next(gsum)
    for _ in wide:
        pass
    copies += store_halves(acol[...], acol_hi, acol_lo, (acol_hi_out, acol_lo_out), (2, 3))

    rows[...] = jnp.zeros_like(rows)
    diag[...] = jnp.zeros_like(diag)
    group = Group(place, links, whole, swapped)
    for block in range(2):
        chunks = pl.ds(4 * block, 4)
        span = pl.ds(TILE // 2 * block, TILE // 2)

        def row_terms(k, carry):
            @pl.when(8 * k + col < row)
            def _():
                right = [ref[pl.ds(8 * k, 8)].reshape(TILE, K) for ref in (acol_hi, acol_lo)]
                rows[chunks] += dot3(split(s[k, span]), right).reshape(4, CHUNK, K)

            return carry

        lax.fori_loop(0, SLOTS, row_terms, 0)

        @pl.when(own)
        def _():
            right = [ref[...].reshape(TILE, K) for ref in (arow_hi, arow_lo)]
            diag[chunks] = dot3(split(s[place.x, span]), right).reshape(4, CHUNK, K)

        whole[chunks] = rows[chunks] + diag[chunks]
        for index in range(4 * block, 4 * block + 4):
            group.send(index)

    terms = (rows[...] + 0.5 * diag[...]).reshape(TILE, K)
    lower = dot3(split(turned[...]), split(terms))
    nvalue[...] = lower.reshape(nvalue.shape)
    nsum = small_sum(place, links, nvalue, nsib, nchips, ndepth, ntotal)
    next(nsum)
    next(tall)
    next(gsum)
    next(nsum)
    group.wait()
    deep = ring_sum(place, links, swapped, zland, zhalf)
    next(deep)
    next(gsum)
    next(deep)
    next(nsum)
    for _ in range(4):
        next(tall)
    for _ in gsum:
        pass
    scaled[...], left, right = scale(gtotal[...].reshape(K, K))
    rest = unit_matrix() - scaled[...]
    square = dot3(split(rest), split(rest))
    close = jnp.sum(square * square) < 0.8
    bound = jnp.max(jnp.sum(jnp.abs(scaled[...]), 1, keepdims=True))
    inverse[...] = jnp.where(close, unit_matrix() + rest, unit_matrix() / bound)
    for _ in deep:
        pass
    for _ in tall:
        pass
    product = part[row] + swapped[col]
    ycol[row] = product

    wide = plane_gather(place, links, ycol, ycol_out)
    next(wide)
    turn = Turn(place, links, yrow_out, own, other)
    for step in range(8):
        piece = mod(col + step, 8)
        device = {"row": base + col, "col": piece}
        turn.start(ycol.at[row], yrow_out.at[inner], device, None if step else other)

    mine = pltpu.make_async_copy(ycol.at[row], yrow_out.at[inner], out_sem.at[10])
    pl.when(own)(mine.start)
    next(nsum)
    inverse[...], _ = refine(scaled[...], inverse[...])
    for _ in range(3):
        next(wide)
    next(nsum)
    inverse[...], _ = refine(scaled[...], inverse[...])
    next(wide)
    inverse[...], _ = refine(scaled[...], inverse[...])
    next(wide)
    inverse[...], final = refine(scaled[...], inverse[...])
    size[...] = jnp.full(size.shape, final, F32)
    next(wide)

    def keep(ref, out, sem):
        copies.append(pltpu.make_async_copy(ref, out, out_sem.at[sem]))
        copies[-1].start()

    for _ in nsum:
        pass
    mix_hi[...], mix_lo[...] = mixing(inverse[...] * left * right, ntotal[...].reshape(K, K))
    ends = ((gtotal, gram_out), (ntotal, lower_out), (mix_hi, mix_hi_out), (mix_lo, mix_lo_out), (size, size_out))
    for index, (ref, out) in enumerate(ends):
        keep(ref, out, 4 + index)
    next(wide)
    for chip in range(16):
        chunk = 2 * chip + place.core
        pltpu.make_async_copy(ycol.at[chunk], ycol_out.at[chunk], out_sem.at[9]).start()
    copies.append(pltpu.make_async_copy(ycol.at[pl.ds(0, 16)], ycol_out.at[pl.ds(0, 16)], out_sem.at[9]))
    turn.wait()
    pl.when(own)(mine.wait)
    for _ in wide:
        pass
    for copy in copies:
        copy.wait()
    links.finish(place.sibling())


def update_kernel(
    stored,
    acol_hi,
    acol_lo,
    arow_hi,
    arow_lo,
    ycol,
    yrow,
    gram_in,
    lower_in,
    mix_hi,
    mix_lo,
    size_in,
    out,
    s,
    ah,
    al,
    rh,
    rl,
    yc,
    yr,
    gn,
    mh,
    ml,
    size,
    scaled,
    inverse,
    load_sem,
    out_sem,
):
    row, col = lax.axis_index("row"), lax.axis_index("col")
    pairs = [(size_in, size), (mix_hi, mh), (mix_lo, ml), (yrow, yr), (arow_hi, rh), (arow_lo, rl)]
    heads = len(pairs)
    for k in range(SLOTS):
        eight = pl.ds(8 * k, 8)
        pairs += [(ref.at[eight], land.at[eight]) for ref, land in ((ycol, yc), (acol_hi, ah), (acol_lo, al))]
        pairs.append((stored.at[:, k, :], s.at[k]))
    loads = [pltpu.make_async_copy(source, land, load_sem.at[index]) for index, (source, land) in enumerate(pairs)]
    for load in loads:
        load.start()
    for load in loads[:heads]:
        load.wait()

    @pl.when(jnp.max(size[...]) > 1e-6)
    def _():
        for index, source in enumerate((gram_in, lower_in)):
            load = pltpu.make_async_copy(source, gn.at[index], out_sem.at[index])
            load.start()
            load.wait()
        scaled[...], left, right = scale(gn[0].reshape(K, K))
        bound = jnp.max(jnp.sum(jnp.abs(scaled[...]), 1, keepdims=True))
        inverse[...] = unit_matrix() / bound

        def again(state):
            count, rest = state
            return (count < 64) & (rest > 1e-6)

        def step(state):
            inverse[...], rest = refine(scaled[...], inverse[...])
            return state[0] + 1, rest

        lax.while_loop(again, step, (jnp.int32(0), jnp.float32(1.0)))
        mh[...], ml[...] = mixing(inverse[...] * left * right, gn[1].reshape(K, K))

    mix = mh[...], ml[...]
    yr_halves = split(yr[...].reshape(TILE, K))
    row_halves = [ref[...].reshape(TILE, K) for ref in (rh, rl)]
    wrow = split(dot3([jnp.concatenate(pair, 1) for pair in zip(yr_halves, row_halves)], mix))
    left_pair = [jnp.concatenate(pair, 1) for pair in zip(row_halves, wrow)]
    stores = [pltpu.make_async_copy(s.at[k], out.at[:, k, :], out_sem.at[k]) for k in range(SLOTS)]

    def tile(k, carry):
        eight = pl.ds(8 * k, 8)
        for index, ref in enumerate((yc.at[eight], ah.at[eight], al.at[eight], s.at[k])):
            pltpu.make_async_copy(ref, ref, load_sem.at[heads + 4 * k + index]).wait()

        @pl.when(8 * k + col == row)
        def _():
            value = s[k]
            down = lax.broadcasted_iota(jnp.int32, (TILE, TILE), 0)
            along = lax.broadcasted_iota(jnp.int32, (TILE, TILE), 1)
            s[k] = jnp.where(down >= along, value, 0.0) + jnp.where(down > along, value, 0.0).T

        @pl.when(8 * k + col > row)
        def _():
            s[k] = jnp.zeros((TILE, TILE), F32)

        @pl.when(8 * k + col <= row)
        def _():
            y_halves = split(yc[eight].reshape(TILE, K))
            a_halves = [ref[eight].reshape(TILE, K) for ref in (ah, al)]
            wcol = split(dot3([jnp.concatenate(pair, 1) for pair in zip(y_halves, a_halves)], mix))
            right_pair = [jnp.concatenate(pair, 1) for pair in zip(wcol, a_halves)]
            s[k] -= dot3(left_pair, right_pair, NT)

        for index in range(SLOTS):
            pl.when(k == index)(stores[index].start)
        return carry

    lax.fori_loop(0, SLOTS, tile, 0)
    for store in stores:
        store.wait()


def body(stored, panel):
    any_spec = pl.BlockSpec(memory_space=pl.ANY)
    vmem, dma = pltpu.VMEM, pltpu.SemaphoreType.DMA
    col_shape, row_shape, square, wide = (32, CHUNK, K), (8, CHUNK, K), (16, 2, 8, K), (2 * K, K)
    out_types = [(col_shape, BF16)] * 2 + [(row_shape, BF16)] * 2 + [(col_shape, F32), (row_shape, F32)]
    out_types += [(square, F32)] * 2 + [(wide, BF16)] * 2 + [((8, 128), F32)]
    small = [
        vmem(square, F32),
        vmem((16, 8, K), F32),
        vmem((16, 8, K), F32),
        vmem((2, 16, 8, K), F32),
        vmem(square, F32),
    ]
    parts = pl.pallas_call(
        exchange_kernel,
        out_shape=[jax.ShapeDtypeStruct(shape, kind) for shape, kind in out_types],
        in_specs=[any_spec] * 2,
        out_specs=[any_spec] * len(out_types),
        scratch_shapes=[
            vmem((SLOTS, TILE, TILE), F32),
            vmem((8, K // 8, TILE), F32),
            vmem((8, 16, 128), F32),
            vmem((8, 16, 128), F32),
            vmem(col_shape, F32),
            vmem((K, TILE), F32),
            vmem(col_shape, BF16),
            vmem(col_shape, BF16),
            vmem(row_shape, BF16),
            vmem(row_shape, BF16),
            vmem(row_shape, F32),
            vmem(row_shape, F32),
            vmem(row_shape, F32),
            vmem(row_shape, F32),
            vmem((2, 3, CHUNK, K), F32),
            vmem((2, CHUNK // 2, K), F32),
            vmem(col_shape, F32),
            vmem((16, CHUNK, K), F32),
            vmem((4, 3, CHUNK, K), F32),
            vmem((3, CHUNK, K), F32),
            vmem(col_shape, F32),
            *small,
            *small,
            vmem((K, K), F32),
            vmem((K, K), F32),
            vmem(wide, BF16),
            vmem(wide, BF16),
            vmem((8, 128), F32),
            dma((SLOTS + 1,)),
            dma((11,)),
            dma((SENDS,)),
            dma((RECVS,)),
        ],
        compiler_params=pltpu.CompilerParams(collective_id=0, has_side_effects=True, vmem_limit_bytes=56 << 20),
        name="exchange",
    )(stored, panel.T)
    return pl.pallas_call(
        update_kernel,
        out_shape=jax.ShapeDtypeStruct(stored.shape, F32),
        in_specs=[any_spec] * (1 + len(out_types)),
        out_specs=any_spec,
        scratch_shapes=[
            vmem((SLOTS, TILE, TILE), F32),
            vmem(col_shape, BF16),
            vmem(col_shape, BF16),
            vmem(row_shape, BF16),
            vmem(row_shape, BF16),
            vmem(col_shape, F32),
            vmem(row_shape, F32),
            vmem((2, *square), F32),
            vmem(wide, BF16),
            vmem(wide, BF16),
            vmem((8, 128), F32),
            vmem((K, K), F32),
            vmem((K, K), F32),
            dma((22,)),
            dma((SLOTS,)),
        ],
        compiler_params=pltpu.CompilerParams(vmem_limit_bytes=56 << 20),
        name="update",
    )(stored, *parts)


def solution(mesh):
    in_specs = (P("row", None, "col"), P("row", "col"))
    out_specs = P("row", None, "col")
    return jax.shard_map(body, mesh=mesh, in_specs=in_specs, out_specs=out_specs, check_vma=False)
```

```python
import functools

import jax
import jax.numpy as jnp
from jax import lax
from jax.experimental import pallas as pl
from jax.experimental.pallas import tpu as pltpu
from jax.sharding import PartitionSpec as P

F32 = jnp.float32
BF16 = jnp.bfloat16
HIGHEST = lax.Precision.HIGHEST
MESH = pl.DeviceIdType.MESH
TILE = 512
K = 256
SLOTS = 4
SENDS, RECVS = 22, 54
CHUNK = 64
NN = (((1,), (0,)), ((), ()))
NT = (((1,), (1,)), ((), ()))


def split(value):
    high = value.astype(BF16)
    return high, (value - high.astype(F32)).astype(BF16)


def dot3(left, right, dims=NN):
    (lh, ll), (rh, rl) = left, right
    dot = functools.partial(lax.dot_general, dimension_numbers=dims, preferred_element_type=F32)
    return dot(lh, rh) + (dot(lh, rl) + dot(ll, rh))


def dot6(left, right, dims=NN):
    return lax.dot_general(left, right, dims, precision=HIGHEST, preferred_element_type=F32)


def mod(value, size):
    return lax.rem(value, size)


class Place:
    def __init__(self):
        self.row = lax.axis_index("row")
        self.col = lax.axis_index("col")
        self.x = lax.div(self.row, 8)
        self.inner = mod(self.row, 8)
        self.y = lax.div(self.inner, 2)
        self.core = mod(self.row, 2)
        self.u = self.y * (1 - self.core) + self.x * self.core
        self.v = self.x * (1 - self.core) + self.y * self.core

    def ring(self, du, dv):
        u, v = mod(self.u + du, 4), mod(self.v + dv, 4)
        return (8 * v + 2 * u) * (1 - self.core) + (8 * u + 2 * v + 1) * self.core

    def at(self, du, dv):
        return {"row": self.ring(du, dv), "col": self.col}

    def sibling(self):
        return {"row": self.row + 1 - 2 * self.core, "col": self.col}

    def up(self, dz):
        return {"row": self.row, "col": mod(self.col + dz % 8, 8)}


class Links:
    def __init__(self, send, recv):
        self.send, self.recv = send, recv
        self.sends, self.slots = 0, 0
        self.ends = []

    def slot(self):
        self.slots += 1
        return self.slots - 1

    def batch(self, ref, when=None):
        self.sends += 1
        self.ends.append((self.sends - 1, ref, when))
        return self.sends - 1

    def copy(self, source, target, slot, device, send):
        return pltpu.make_async_remote_copy(
            src_ref=source,
            dst_ref=target,
            send_sem=self.send.at[send],
            recv_sem=self.recv.at[slot],
            device_id=device,
            device_id_type=MESH,
        )

    def start(self, source, target, slot, device, send=None, when=None):
        send = self.batch(source) if send is None else send
        copy = self.copy(source, target, slot, device, send)
        copy.start() if when is None else pl.when(when)(copy.start)

    def wait(self, ref, slot, device, when=None):
        copy = self.copy(ref, ref, slot, device, 0)
        copy.wait_recv() if when is None else pl.when(when)(copy.wait_recv)

    def finish(self, device):
        for send, ref, when in self.ends:
            copy = self.copy(ref, ref, 0, device, send)
            copy.wait_send() if when is None else pl.when(when)(copy.wait_send)


def plane_gather(place, links, buf, kept=None):
    kept = buf if kept is None else kept
    near = [None] + [links.slot() for _ in range(3)]
    far = [links.slot() for _ in range(4)]
    across = links.slot()
    batch = links.batch(buf.at[pl.ds(0, 31)])

    def send(du, dv, slot, device):
        ref = buf.at[place.ring(du, dv)]
        links.start(ref, ref, slot, device, batch)

    def hand_over(du, dv):
        chunk = place.ring(du, dv)
        links.start(buf.at[chunk], kept.at[chunk], across, place.sibling(), batch)

    def spread(du):
        for way in (2, 1, 3):
            send(du, 0, far[du], place.at(0, way))
        hand_over(du, 0)

    for way in (2, 1, 3):
        send(0, 0, near[way], place.at(way, 0))
    spread(0)
    yield
    for way in (1, 3, 2):
        links.wait(buf.at[place.ring(4 - way, 0)], near[way], place.at(4 - way, 0))
        spread(4 - way)
        yield
    for du in (0, 3, 1, 2):
        links.wait(buf.at[pl.ds(0, 3)], far[du], place.at(0, 1))
        for way in (1, 3, 2):
            hand_over(du, way)
        yield
    links.wait(kept.at[pl.ds(0, 16)], across, place.sibling())


def plane_sum(place, links, buf, sib, vland, uland):
    sib_slots = [links.slot() for _ in range(SLOTS)]
    vs = [links.slot() for _ in range(4)]
    us = links.slot()
    batch = links.batch(buf.at[pl.ds(0, 31)])
    for tile in range(SLOTS):
        for y in range(4):
            links.start(
                buf.at[8 * tile + 2 * y + 1 - place.core],
                sib.at[4 * tile + y],
                sib_slots[tile],
                place.sibling(),
                batch,
            )
        yield
    for tile in range(SLOTS):
        links.wait(sib.at[pl.ds(4 * tile, 4)], sib_slots[tile], place.sibling())
        for y in range(4):
            buf[8 * tile + 2 * y + place.core] += sib[4 * tile + y]
    order = (2, 1, 3, 0)
    for core in range(2):
        for du in order:
            for way in (2, 1, 3):
                links.start(
                    buf.at[place.ring(du, way)],
                    vland.at[du, way - 1],
                    vs[du],
                    place.at(0, way),
                    batch,
                    place.core == core,
                )
        yield
    for du in order:
        links.wait(vland.at[du], vs[du], place.at(0, 1))
        chunk = place.ring(du, 0)
        buf[chunk] += vland[du, 0] + (vland[du, 1] + vland[du, 2])
        if du:
            links.start(buf.at[chunk], uland.at[du - 1], us, place.at(du, 0), batch)
        yield
    links.wait(uland, us, place.at(1, 0))
    buf[place.ring(0, 0)] += uland[0] + (uland[1] + uland[2])


def small_sum(place, links, value, sib, chips, depth, total):
    chip = lax.div(place.row, 2)
    sib_slot, chip_slot, depth_slot, back_slot, last_slot = [links.slot() for _ in range(5)]

    def peer(step):
        index = mod(chip + step, 16)
        return index, {"row": 2 * index + place.core, "col": place.col}

    links.start(value.at[:, 1 - place.core], sib, sib_slot, place.sibling())
    yield
    links.wait(sib, sib_slot, place.sibling())
    for index in range(16):
        chips[index] = value[index, place.core] + sib[index]
    batch = links.batch(chips.at[pl.ds(0, 15)])
    for step in range(1, 16):
        index, device = peer(step)
        links.start(chips.at[index], depth.at[0, chip], chip_slot, device, batch)
    yield
    links.wait(depth.at[0, pl.ds(0, 15)], chip_slot, place.sibling())
    depth[0, chip] = chips[chip]
    depth[1, place.col] = jnp.sum(depth[0], 0)
    batch = links.batch(depth.at[1, pl.ds(0, 7)])
    for step in range(1, 8):
        links.start(depth.at[1, place.col], depth.at[1, place.col], depth_slot, place.up(step), batch)
    yield
    links.wait(depth.at[1, pl.ds(0, 7)], depth_slot, place.up(1))
    total[chip, place.core] = jnp.sum(depth[1, :8], 0)
    own = total.at[chip, place.core]
    batch = links.batch(total.at[pl.ds(0, 15), place.core])
    for step in range(1, 16):
        links.start(own, own, back_slot, peer(step)[1], batch)
    yield
    links.wait(total.at[pl.ds(0, 15), place.core], back_slot, place.sibling())
    links.start(total.at[:, place.core], total.at[:, place.core], last_slot, place.sibling())
    yield
    links.wait(total.at[:, 1 - place.core], last_slot, place.sibling())


def ring_gather(place, links, buf):
    rows = buf.shape[1]
    part = (pl.ds(0, rows // 2), pl.ds(rows // 2, rows // 2))
    one, two, three, four = [(links.slot(), links.slot()) for _ in range(4)]
    wholes, halves = links.batch(buf.at[pl.ds(0, 6)]), links.batch(buf.at[0])
    ways = ((0, 1), (1, -1))

    def piece(offset):
        return buf.at[mod(place.col + offset % 8, 8)]

    def half(offset, which):
        return buf.at[mod(place.col + offset % 8, 8), part[which]]

    for which, way in ways:
        links.start(piece(0), piece(0), two[which], place.up(2 * way), wholes)
    for which, way in ways:
        links.start(piece(0), piece(0), one[which], place.up(way), wholes)
    yield
    for which, way in ways:
        source = piece(-2 * way)
        links.wait(source, two[which], place.up(-2 * way))
        links.start(half(-2 * way, which), half(-2 * way, which), four[which], place.up(2 * way), halves)
        links.start(source, source, three[which], place.up(way), wholes)
    yield
    for which, way in ways:
        links.wait(piece(-way), one[which], place.up(-way))
        links.wait(piece(-3 * way), three[which], place.up(-way))
        links.wait(half(-4 * way, which), four[which], place.up(-2 * way))


def ring_sum(place, links, buf, land, half_land):
    rows = buf.shape[1]
    part = (pl.ds(0, rows // 2), pl.ds(rows // 2, rows // 2))
    one, two, three, four = [(links.slot(), links.slot()) for _ in range(4)]
    wholes, halves = links.batch(buf.at[pl.ds(0, 6)]), links.batch(buf.at[0])
    ways = ((0, 1), (1, -1))

    def piece(offset):
        return mod(place.col + offset % 8, 8)

    for which, way in ways:
        links.start(buf.at[piece(4 * way), part[which]], half_land.at[which], four[which], place.up(2 * way), halves)
        links.start(buf.at[piece(3 * way)], land.at[which, 2], three[which], place.up(way), wholes)
    for which, way in ways:
        links.start(buf.at[piece(way)], land.at[which, 0], one[which], place.up(way), wholes)
    yield
    for which, way in ways:
        links.wait(land.at[which, 2], three[which], place.up(-way))
        links.wait(half_land.at[which], four[which], place.up(-2 * way))
        index = piece(2 * way)
        buf[index] += land[which, 2]
        buf[index, part[which]] += half_land[which]
        links.start(buf.at[index], land.at[which, 1], two[which], place.up(2 * way), wholes)
    yield
    for which, way in ways:
        links.wait(land.at[which, 0], one[which], place.up(-way))
        links.wait(land.at[which, 1], two[which], place.up(-2 * way))
    buf[place.col] += (land[0, 0] + land[1, 0]) + (land[0, 1] + land[1, 1])


class Group:
    def __init__(self, place, links, source, target):
        self.place, self.links, self.source, self.target = place, links, source, target
        self.slot = links.slot()
        self.batch = links.batch(target.at[pl.ds(0, 7)])

    def send(self, index):
        place = self.place
        here = place.inner == index

        @pl.when(here)
        def _():
            self.target[place.inner] = self.source[index]

        device = {"row": place.row - place.inner + index, "col": place.col}
        self.links.start(
            self.source.at[index], self.target.at[place.inner], self.slot, device, self.batch, jnp.logical_not(here)
        )

    def wait(self):
        self.links.wait(self.target.at[pl.ds(0, 7)], self.slot, self.place.sibling())


class Turn:
    def __init__(self, place, links, target, own, other):
        self.place, self.links, self.target, self.own, self.other = place, links, target, own, other
        self.slot = links.slot()
        self.batches = links.batch(target.at[pl.ds(0, 7)], own), links.batch(target.at[pl.ds(0, 8)], other)

    def start(self, source, target, device, when):
        for batch, side in zip(self.batches, (self.own, self.other)):
            if when is None:
                self.links.start(source, target, self.slot, device, batch, side)
            elif side is self.other:
                self.links.start(source, target, self.slot, device, batch, side)

    def wait(self):
        self.links.wait(self.target.at[pl.ds(0, 7)], self.slot, self.place.sibling(), self.own)
        self.links.wait(self.target.at[pl.ds(0, 8)], self.slot, self.place.sibling(), self.other)


def unit_matrix():
    return jnp.where(
        lax.broadcasted_iota(jnp.int32, (K, K), 0) == lax.broadcasted_iota(jnp.int32, (K, K), 1), 1.0, 0.0
    ).astype(F32)


def scale(gram):
    diagonal = gram * unit_matrix()
    left = lax.rsqrt(jnp.sum(diagonal, 1, keepdims=True))
    right = lax.rsqrt(jnp.sum(diagonal, 0, keepdims=True))
    return gram * left * right, left, right


def refine(scaled, inverse):
    rest = unit_matrix() - dot6(scaled, inverse)
    return inverse + dot3(split(inverse), split(rest)), jnp.sum(rest * rest)


def mixing(inverse, lower):
    halves = split(inverse)
    twist = dot3(halves, split(dot3(split(lower + lower.T), halves)))
    return split(jnp.concatenate([2.0 * inverse, -2.0 * twist], 0))


def pack(slab, pieces):
    low = lax.broadcasted_iota(jnp.int32, (16, 128), 1) < CHUNK
    for pair in range(4):
        first, second = [slab[16 * side : 16 * side + 16, 128 * pair : 128 * pair + 128] for side in range(2)]
        pieces[2 * pair] = jnp.where(low, first, pltpu.roll(second, CHUNK, 1))
        pieces[2 * pair + 1] = jnp.where(low, pltpu.roll(first, CHUNK, 1), second)


def unpack(pieces):
    turned = pieces.reshape(128, 128).T
    return jnp.concatenate([turned[:CHUNK], turned[CHUNK:]], 1)


def unpack_row(slabs):
    return jnp.concatenate([slabs[index, 16 * side : 16 * side + 16, :] for side in range(2) for index in range(8)], 0)


def exchange_kernel(
    stored,
    panel,
    acol_hi_out,
    acol_lo_out,
    arow_hi_out,
    arow_lo_out,
    ycol_out,
    yrow_out,
    gram_out,
    lower_out,
    mix_hi_out,
    mix_lo_out,
    size_out,
    s,
    slabs,
    packed,
    colpk,
    acol,
    turned,
    acol_hi,
    acol_lo,
    arow_hi,
    arow_lo,
    rows,
    diag,
    whole,
    swapped,
    zland,
    zhalf,
    part,
    sib,
    vland,
    uland,
    ycol,
    gvalue,
    gsib,
    gchips,
    gdepth,
    gtotal,
    nvalue,
    nsib,
    nchips,
    ndepth,
    ntotal,
    scaled,
    inverse,
    mix_hi,
    mix_lo,
    size,
    load_sem,
    out_sem,
    send_sem,
    recv_sem,
):
    place = Place()
    links = Links(send_sem, recv_sem)
    row, col, inner = place.row, place.col, place.inner
    base = row - inner
    fetch = pltpu.make_async_copy(panel, slabs.at[col], load_sem.at[SLOTS])
    fetch.start()
    loads = [pltpu.make_async_copy(stored.at[:, k, :], s.at[k], load_sem.at[k]) for k in range(SLOTS)]
    for load in loads:
        load.start()

    barrier = pltpu.get_barrier_semaphore()

    def greet(device):
        pl.semaphore_signal(barrier, inc=1, device_id=device, device_id_type=MESH)

    own = inner == col
    other = jnp.logical_not(own)
    for step in range(1, 8):
        greet({"row": base + mod(inner + step, 8), "col": inner})
        greet({"row": base + col, "col": mod(col + step, 8)})
        greet(place.up(step))
        greet({"row": base + mod(inner + step, 8), "col": col})
    for step in range(1, 16):
        greet({"row": mod(row + 2 * step, 32), "col": col})

    @pl.when(other)
    def _():
        greet({"row": row, "col": inner})
        greet({"row": base + col, "col": col})

    fetch.wait()
    pack(slabs[col], packed)
    pl.when(own)(lambda: pl.semaphore_wait(barrier, 43))
    pl.when(other)(lambda: pl.semaphore_wait(barrier, 45))

    turn = Turn(place, links, colpk, own, other)
    for step in range(8):
        piece = mod(inner + step, 8)
        device = {"row": base + piece, "col": inner}
        turn.start(packed.at[piece], colpk.at[col], device, None if step else other)
    deep = ring_gather(place, links, slabs)
    next(deep)

    @pl.when(own)
    def _():
        colpk[col] = packed[inner]

    for load in loads:
        load.wait()

    @pl.when(own)
    def _():
        value = s[place.x]
        below = lax.broadcasted_iota(jnp.int32, (TILE, TILE), 0)
        across = lax.broadcasted_iota(jnp.int32, (TILE, TILE), 1)
        s[place.x] = jnp.where(below >= across, value, 0.0) + jnp.where(below > across, value, 0.0).T

    next(deep)
    turn.wait()
    acol[row] = unpack(colpk[...])
    wide = plane_gather(place, links, acol)
    next(wide)
    chunk = acol[row]
    gvalue[...] = dot6(chunk.T, chunk).reshape(gvalue.shape)
    gsum = small_sum(place, links, gvalue, gsib, gchips, gdepth, gtotal)
    next(gsum)
    for _ in deep:
        pass
    for _ in range(3):
        next(wide)

    def store_halves(source, high, low, outs, sems):
        high[...], low[...] = split(source)
        copies = [pltpu.make_async_copy(ref, out, out_sem.at[sem]) for ref, out, sem in zip((high, low), outs, sems)]
        for copy in copies:
            copy.start()
        return copies

    turned[...] = unpack_row(slabs[...])
    copies = store_halves(turned[...].T.reshape(8, CHUNK, K), arow_hi, arow_lo, (arow_hi_out, arow_lo_out), (0, 1))
    next(gsum)
    next(wide)

    tall = plane_sum(place, links, part, sib, vland, uland)
    for k in range(SLOTS):
        part[8 * k : 8 * k + 8] = jnp.zeros((8, CHUNK, K), F32)

        @pl.when(8 * k + col < row)
        def _():
            terms = dot3(split(s[k].T), [ref[...].reshape(TILE, K) for ref in (arow_hi, arow_lo)])
            part[8 * k : 8 * k + 8] = terms.reshape(8, CHUNK, K)

        next(tall)
        if k < 2:
            next(wide)
    next(wide)
    next(tall)
    next(gsum)
    for _ in wide:
        pass
    copies += store_halves(acol[...], acol_hi, acol_lo, (acol_hi_out, acol_lo_out), (2, 3))

    rows[...] = jnp.zeros_like(rows)
    diag[...] = jnp.zeros_like(diag)
    group = Group(place, links, whole, swapped)
    for block in range(2):
        chunks = pl.ds(4 * block, 4)
        span = pl.ds(TILE // 2 * block, TILE // 2)

        def row_terms(k, carry):
            @pl.when(8 * k + col < row)
            def _():
                right = [ref[pl.ds(8 * k, 8)].reshape(TILE, K) for ref in (acol_hi, acol_lo)]
                rows[chunks] += dot3(split(s[k, span]), right).reshape(4, CHUNK, K)

            return carry

        lax.fori_loop(0, SLOTS, row_terms, 0)

        @pl.when(own)
        def _():
            right = [ref[...].reshape(TILE, K) for ref in (arow_hi, arow_lo)]
            diag[chunks] = dot3(split(s[place.x, span]), right).reshape(4, CHUNK, K)

        whole[chunks] = rows[chunks] + diag[chunks]
        for index in range(4 * block, 4 * block + 4):
            group.send(index)

    terms = (rows[...] + 0.5 * diag[...]).reshape(TILE, K)
    lower = dot3(split(turned[...]), split(terms))
    nvalue[...] = lower.reshape(nvalue.shape)
    nsum = small_sum(place, links, nvalue, nsib, nchips, ndepth, ntotal)
    next(nsum)
    next(tall)
    next(gsum)
    next(nsum)
    group.wait()
    deep = ring_sum(place, links, swapped, zland, zhalf)
    next(deep)
    next(gsum)
    next(deep)
    next(nsum)
    for _ in range(4):
        next(tall)
    for _ in gsum:
        pass
    scaled[...], left, right = scale(gtotal[...].reshape(K, K))
    rest = unit_matrix() - scaled[...]
    square = dot3(split(rest), split(rest))
    close = jnp.sum(square * square) < 0.8
    bound = jnp.max(jnp.sum(jnp.abs(scaled[...]), 1, keepdims=True))
    inverse[...] = jnp.where(close, unit_matrix() + rest, unit_matrix() / bound)
    for _ in deep:
        pass
    for _ in tall:
        pass
    product = part[row] + swapped[col]
    ycol[row] = product

    wide = plane_gather(place, links, ycol, ycol_out)
    next(wide)
    turn = Turn(place, links, yrow_out, own, other)
    for step in range(8):
        piece = mod(col + step, 8)
        device = {"row": base + col, "col": piece}
        turn.start(ycol.at[row], yrow_out.at[inner], device, None if step else other)

    mine = pltpu.make_async_copy(ycol.at[row], yrow_out.at[inner], out_sem.at[10])
    pl.when(own)(mine.start)
    next(nsum)
    inverse[...], _ = refine(scaled[...], inverse[...])
    for _ in range(3):
        next(wide)
    next(nsum)
    inverse[...], _ = refine(scaled[...], inverse[...])
    next(wide)
    inverse[...], _ = refine(scaled[...], inverse[...])
    next(wide)
    inverse[...], final = refine(scaled[...], inverse[...])
    size[...] = jnp.full(size.shape, final, F32)
    next(wide)

    def keep(ref, out, sem):
        copies.append(pltpu.make_async_copy(ref, out, out_sem.at[sem]))
        copies[-1].start()

    for _ in nsum:
        pass
    mix_hi[...], mix_lo[...] = mixing(inverse[...] * left * right, ntotal[...].reshape(K, K))
    ends = ((gtotal, gram_out), (ntotal, lower_out), (mix_hi, mix_hi_out), (mix_lo, mix_lo_out), (size, size_out))
    for index, (ref, out) in enumerate(ends):
        keep(ref, out, 4 + index)
    next(wide)
    for chip in range(16):
        chunk = 2 * chip + place.core
        pltpu.make_async_copy(ycol.at[chunk], ycol_out.at[chunk], out_sem.at[9]).start()
    copies.append(pltpu.make_async_copy(ycol.at[pl.ds(0, 16)], ycol_out.at[pl.ds(0, 16)], out_sem.at[9]))
    turn.wait()
    pl.when(own)(mine.wait)
    for _ in wide:
        pass
    for copy in copies:
        copy.wait()
    links.finish(place.sibling())


def update_kernel(
    stored,
    acol_hi,
    acol_lo,
    arow_hi,
    arow_lo,
    ycol,
    yrow,
    gram_in,
    lower_in,
    mix_hi,
    mix_lo,
    size_in,
    out,
    s,
    ah,
    al,
    rh,
    rl,
    yc,
    yr,
    gn,
    mh,
    ml,
    size,
    scaled,
    inverse,
    load_sem,
    out_sem,
):
    row, col = lax.axis_index("row"), lax.axis_index("col")
    pairs = [(size_in, size), (mix_hi, mh), (mix_lo, ml), (yrow, yr), (arow_hi, rh), (arow_lo, rl)]
    heads = len(pairs)
    for k in range(SLOTS):
        eight = pl.ds(8 * k, 8)
        pairs += [(ref.at[eight], land.at[eight]) for ref, land in ((ycol, yc), (acol_hi, ah), (acol_lo, al))]
        pairs.append((stored.at[:, k, :], s.at[k]))
    loads = [pltpu.make_async_copy(source, land, load_sem.at[index]) for index, (source, land) in enumerate(pairs)]
    for load in loads:
        load.start()
    for load in loads[:heads]:
        load.wait()

    @pl.when(jnp.max(size[...]) > 1e-6)
    def _():
        for index, source in enumerate((gram_in, lower_in)):
            load = pltpu.make_async_copy(source, gn.at[index], out_sem.at[index])
            load.start()
            load.wait()
        scaled[...], left, right = scale(gn[0].reshape(K, K))
        bound = jnp.max(jnp.sum(jnp.abs(scaled[...]), 1, keepdims=True))
        inverse[...] = unit_matrix() / bound

        def again(state):
            count, rest = state
            return (count < 64) & (rest > 1e-6)

        def step(state):
            inverse[...], rest = refine(scaled[...], inverse[...])
            return state[0] + 1, rest

        lax.while_loop(again, step, (jnp.int32(0), jnp.float32(1.0)))
        mh[...], ml[...] = mixing(inverse[...] * left * right, gn[1].reshape(K, K))

    mix = mh[...], ml[...]
    yr_halves = split(yr[...].reshape(TILE, K))
    row_halves = [ref[...].reshape(TILE, K) for ref in (rh, rl)]
    wrow = split(dot3([jnp.concatenate(pair, 1) for pair in zip(yr_halves, row_halves)], mix))
    left_pair = [jnp.concatenate(pair, 1) for pair in zip(row_halves, wrow)]
    stores = [pltpu.make_async_copy(s.at[k], out.at[:, k, :], out_sem.at[k]) for k in range(SLOTS)]

    def tile(k, carry):
        eight = pl.ds(8 * k, 8)
        for index, ref in enumerate((yc.at[eight], ah.at[eight], al.at[eight], s.at[k])):
            pltpu.make_async_copy(ref, ref, load_sem.at[heads + 4 * k + index]).wait()

        @pl.when(8 * k + col == row)
        def _():
            value = s[k]
            down = lax.broadcasted_iota(jnp.int32, (TILE, TILE), 0)
            along = lax.broadcasted_iota(jnp.int32, (TILE, TILE), 1)
            s[k] = jnp.where(down >= along, value, 0.0) + jnp.where(down > along, value, 0.0).T

        @pl.when(8 * k + col > row)
        def _():
            s[k] = jnp.zeros((TILE, TILE), F32)

        @pl.when(8 * k + col <= row)
        def _():
            y_halves = split(yc[eight].reshape(TILE, K))
            a_halves = [ref[eight].reshape(TILE, K) for ref in (ah, al)]
            wcol = split(dot3([jnp.concatenate(pair, 1) for pair in zip(y_halves, a_halves)], mix))
            right_pair = [jnp.concatenate(pair, 1) for pair in zip(wcol, a_halves)]
            s[k] -= dot3(left_pair, right_pair, NT)

        for index in range(SLOTS):
            pl.when(k == index)(stores[index].start)
        return carry

    lax.fori_loop(0, SLOTS, tile, 0)
    for store in stores:
        store.wait()


def body(stored, panel):
    any_spec = pl.BlockSpec(memory_space=pl.ANY)
    vmem, dma = pltpu.VMEM, pltpu.SemaphoreType.DMA
    col_shape, row_shape, square, wide = (32, CHUNK, K), (8, CHUNK, K), (16, 2, 8, K), (2 * K, K)
    out_types = [(col_shape, BF16)] * 2 + [(row_shape, BF16)] * 2 + [(col_shape, F32), (row_shape, F32)]
    out_types += [(square, F32)] * 2 + [(wide, BF16)] * 2 + [((8, 128), F32)]
    small = [
        vmem(square, F32),
        vmem((16, 8, K), F32),
        vmem((16, 8, K), F32),
        vmem((2, 16, 8, K), F32),
        vmem(square, F32),
    ]
    parts = pl.pallas_call(
        exchange_kernel,
        out_shape=[jax.ShapeDtypeStruct(shape, kind) for shape, kind in out_types],
        in_specs=[any_spec] * 2,
        out_specs=[any_spec] * len(out_types),
        scratch_shapes=[
            vmem((SLOTS, TILE, TILE), F32),
            vmem((8, K // 8, TILE), F32),
            vmem((8, 16, 128), F32),
            vmem((8, 16, 128), F32),
            vmem(col_shape, F32),
            vmem((K, TILE), F32),
            vmem(col_shape, BF16),
            vmem(col_shape, BF16),
            vmem(row_shape, BF16),
            vmem(row_shape, BF16),
            vmem(row_shape, F32),
            vmem(row_shape, F32),
            vmem(row_shape, F32),
            vmem(row_shape, F32),
            vmem((2, 3, CHUNK, K), F32),
            vmem((2, CHUNK // 2, K), F32),
            vmem(col_shape, F32),
            vmem((16, CHUNK, K), F32),
            vmem((4, 3, CHUNK, K), F32),
            vmem((3, CHUNK, K), F32),
            vmem(col_shape, F32),
            *small,
            *small,
            vmem((K, K), F32),
            vmem((K, K), F32),
            vmem(wide, BF16),
            vmem(wide, BF16),
            vmem((8, 128), F32),
            dma((SLOTS + 1,)),
            dma((11,)),
            dma((SENDS,)),
            dma((RECVS,)),
        ],
        compiler_params=pltpu.CompilerParams(collective_id=0, has_side_effects=True, vmem_limit_bytes=56 << 20),
        name="exchange",
    )(stored, panel.T)
    return pl.pallas_call(
        update_kernel,
        out_shape=jax.ShapeDtypeStruct(stored.shape, F32),
        in_specs=[any_spec] * (1 + len(out_types)),
        out_specs=any_spec,
        scratch_shapes=[
            vmem((SLOTS, TILE, TILE), F32),
            vmem(col_shape, BF16),
            vmem(col_shape, BF16),
            vmem(row_shape, BF16),
            vmem(row_shape, BF16),
            vmem(col_shape, F32),
            vmem(row_shape, F32),
            vmem((2, *square), F32),
            vmem(wide, BF16),
            vmem(wide, BF16),
            vmem((8, 128), F32),
            vmem((K, K), F32),
            vmem((K, K), F32),
            dma((22,)),
            dma((SLOTS,)),
        ],
        compiler_params=pltpu.CompilerParams(vmem_limit_bytes=56 << 20),
        name="update",
    )(stored, *parts)


def solution(mesh):
    in_specs = (P("row", None, "col"), P("row", "col"))
    out_specs = P("row", None, "col")
    return jax.shard_map(body, mesh=mesh, in_specs=in_specs, out_specs=out_specs, check_vma=False)
```
